32 devices in a mesh: groups: 2 (over y), dp: 4 (over z), tensor: 4 (over x, core).
Axes of the slice: x: 2, y: 2, z: 4, core: 2. Of those that a mesh axis runs over, the one named last changes fastest.
Arguments:
- queries: bfloat16 [1024, 8192], P(('groups', 'dp'), 'tensor'), parts along dimension 0, may hold values from -36 to 36
- new_keys: bfloat16 [1024, 1024], P(('groups', 'dp'), 'tensor'), parts along dimension 0, may hold values from -6 to 6
- new_values: bfloat16 [1024, 1024], P(('groups', 'dp'), 'tensor'), parts along dimension 0, may hold values from -6 to 6
- key_cache: bfloat16 [1024, 96, 1024], P(('groups', 'dp'), None, 'tensor'), parts along dimension 0, may hold values from -6 to 6
- value_cache: bfloat16 [1024, 96, 1024], P(('groups', 'dp'), None, 'tensor'), parts along dimension 0, may hold values from -6 to 6
- lengths: int32 [1024], P(('groups', 'dp')), parts along dimension 0, may hold values from 2 to 96, as said below
- out_weight: bfloat16 [8192, 4096], P('tensor'), may hold values from -0.0625 to 0.0625
- down_factors: bfloat16 [12, 8192, 64], P('dp', 'tensor'), may hold values from -0.0625 to 0.0625
- up_factors: bfloat16 [12, 64, 4096], P('dp', None, 'tensor'), may hold values from -0.75 to 0.75
- assignment: int32 [1024], P(('groups', 'dp')), parts along dimension 0, may hold values from 0 to 11, as said below
- home_index: int32 [12], replicated, may hold values from 0 to 11, each once
Outputs:
- mixed: bfloat16 [1024, 4096], P(('groups', 'dp')), parts along dimension 0
The draws below stay inside these ranges and needn't reach their ends.
There are 2 independent parts, one for each index of `groups`. The reference program is written for one: setup_inputs(seed, part) draws one part's arguments, and reference() takes and returns one part's arrays. A program takes and returns all parts, laid end to end along the dimension named above; an argument that names none is the same for every part. Nothing has to cross between parts.
Inputs may be any that keep to these rules, and one draw needn't show every extreme that they name: `assignment`: among the 128 requests of one index of dp no variant appears more than 26 times, and one variant appears exactly 26 times among the requests of every index of dp. `home_index`: each storage position once. `lengths`: some request of every index of dp has all 96 positions valid.
All inputs are finite; a program needn't handle non-finite values.
Results may differ from the reference program's by a relative error of at most 0.0085.
Values may be sent and summed in bfloat16 or wider, within the bound.
No kernel may reach another device: no remote copies, remote signals or barrier semaphores. Data moves between devices by JAX's collectives and lax.ppermute only.
A program may use at most 128 MiB of HBM per device.

```python
import math
import jax
import jax.numpy as jnp
from jax import lax

HEADS = 64
KV_HEADS = 8
HEAD_DIM = 128
DW = 4096
RANK = 64
REQ_DEV = 128
CACHE = 96
REQS = 512
VARIANTS = 12
CAP = 26


def draw_queries(key, part):
    key = jax.random.fold_in(key, 11)
    values = jnp.clip(jax.random.normal(key, (REQS, HEADS * HEAD_DIM), jnp.float32), -6.0, 6.0)
    return values.astype(jnp.bfloat16)


def draw_key_cache(key, part):
    key = jax.random.fold_in(key, 12)
    shape = (REQS, CACHE, KV_HEADS * HEAD_DIM)
    values = jnp.clip(jax.random.normal(key, shape, jnp.float32), -6.0, 6.0)
    return values.astype(jnp.bfloat16)


def draw_lengths(key, part):
    key = jax.random.fold_in(key, 13)
    first_key, second_key = jax.random.split(key)
    blocks = REQS // REQ_DEV
    drawn = jax.random.randint(first_key, (REQS,), 2, CACHE + 1, dtype=jnp.int32)
    chosen = jax.random.randint(second_key, (blocks,), 0, REQ_DEV, dtype=jnp.int32)
    within = jnp.arange(REQS, dtype=jnp.int32) % REQ_DEV
    filled = within == jnp.repeat(chosen, REQ_DEV)
    return jnp.where(filled, CACHE, drawn).astype(jnp.int32)


def draw_assignment(key, part):
    key = jax.random.fold_in(key, 14)
    hot_key, rest_key = jax.random.split(key)
    blocks = REQS // REQ_DEV
    hottest = jax.random.randint(hot_key, (), 0, VARIANTS, dtype=jnp.int32)

    def one_block(block_key):
        pick_key, order_key = jax.random.split(block_key)
        spare = jax.random.permutation(pick_key, (VARIANTS - 1) * CAP)[:REQ_DEV - CAP]
        others = (spare // CAP).astype(jnp.int32)
        others = others + (others >= hottest).astype(jnp.int32)
        joined = jnp.concatenate([jnp.full((CAP,), hottest, dtype=jnp.int32), others])
        return jax.random.permutation(order_key, joined).astype(jnp.int32)
    return jax.vmap(one_block)(jax.random.split(rest_key, blocks)).reshape(REQS)


def block_scale(rng, shape, cuts, least, largest):
    gain, own = 1.0, jax.random.fold_in(rng, 6)
    for dim, parts in cuts:
        steps = jnp.exp(jax.random.uniform(jax.random.fold_in(own, dim), (parts,), jnp.float32, least / len(cuts), largest / len(cuts)))
        gain = gain * jnp.repeat(steps, shape[dim] // parts).reshape([-1 if axis == dim else 1 for axis in range(len(shape))])
    return gain


def bell_draw(key, shape, width, reach, cuts=(), kind=jnp.bfloat16):
    values = jax.random.normal(key, shape, jnp.float32) * width
    if len(cuts) > 0:
        values = block_scale(key, shape, cuts, -0.22, 0.18) * values
    return jnp.clip(values, min=-reach, max=reach).astype(kind)


def setup_inputs(seed: int = 0, part: int = 0) -> dict:
    key_list = jax.random.split(jax.random.key(seed), 12)
    part_keys = jax.random.split(jax.random.fold_in(key_list[11], part), 12)
    queries = draw_queries(jax.random.fold_in(jax.random.fold_in(key_list[11], part), 71), part)
    new_keys = bell_draw(part_keys[1], (REQS, KV_HEADS * HEAD_DIM), 1.0, 6.0, ((0, 4), (1, 4)))
    new_values = bell_draw(part_keys[2], (REQS, KV_HEADS * HEAD_DIM), 1.0, 6.0, ((0, 4), (1, 4)))
    key_cache = draw_key_cache(jax.random.fold_in(jax.random.fold_in(key_list[11], part), 71), part)
    value_cache = bell_draw(part_keys[4], (REQS, CACHE, KV_HEADS * HEAD_DIM), 1.0, 6.0, ((0, 4), (2, 4)))
    lengths = draw_lengths(jax.random.fold_in(jax.random.fold_in(key_list[11], part), 71), part)
    out_weight = bell_draw(key_list[6], (HEADS * HEAD_DIM, DW), (HEADS * HEAD_DIM) ** -0.5, 0.0625, ((0, 4),))
    down_factors = bell_draw(key_list[7], (VARIANTS, HEADS * HEAD_DIM, RANK), (HEADS * HEAD_DIM) ** -0.5, 0.0625, ((0, 4), (1, 4)))
    up_factors = bell_draw(key_list[8], (VARIANTS, RANK, DW), RANK ** -0.5, 0.75, ((0, 4), (2, 4)))
    assignment = draw_assignment(jax.random.fold_in(jax.random.fold_in(key_list[11], part), 71), part)
    home_index = jax.random.permutation(key_list[10], VARIANTS).astype(jnp.int32)
    return {"queries": queries, "new_keys": new_keys, "new_values": new_values, "key_cache": key_cache, "value_cache": value_cache, "lengths": lengths, "out_weight": out_weight, "down_factors": down_factors, "up_factors": up_factors, "assignment": assignment, "home_index": home_index}


def attend_block(block):
    queries, new_keys, new_values, key_cache, value_cache, lengths = block
    row_count = queries.shape[0]
    per_group = HEADS // KV_HEADS
    grouped = queries.astype(jnp.float32).reshape(row_count, KV_HEADS, per_group, HEAD_DIM)
    cache_keys = key_cache.astype(jnp.float32).reshape(row_count, CACHE, KV_HEADS, HEAD_DIM)
    cache_values = value_cache.astype(jnp.float32).reshape(row_count, CACHE, KV_HEADS, HEAD_DIM)
    fresh_key = new_keys.astype(jnp.float32).reshape(row_count, KV_HEADS, HEAD_DIM)
    fresh_value = new_values.astype(jnp.float32).reshape(row_count, KV_HEADS, HEAD_DIM)
    score_scale = 1.0 / math.sqrt(HEAD_DIM)
    scores = jnp.einsum('rkgd,rckd->rkgc', grouped, cache_keys) * score_scale
    usable = jnp.arange(CACHE, dtype=jnp.int32)[None, :] < lengths[:, None]
    scores = jnp.where(usable[:, None, None, :], scores, -1e+30)
    own_score = jnp.einsum('rkgd,rkd->rkg', grouped, fresh_key) * score_scale
    highest = jnp.maximum(lax.optimization_barrier(jnp.max(scores, axis=-1)), own_score)
    weights_raw = jnp.exp(scores - highest[..., None])
    own_raw = jnp.exp(own_score - highest)
    denominator = lax.optimization_barrier(jnp.sum(weights_raw, axis=-1)) + own_raw
    weights = (weights_raw / denominator[..., None]).astype(jnp.bfloat16)
    own_weight = (own_raw / denominator).astype(jnp.bfloat16)
    result = jnp.einsum('rkgc,rckd->rkgd', weights.astype(jnp.float32), cache_values)
    result = result + own_weight.astype(jnp.float32)[..., None] * fresh_value[:, :, None, :]
    return result.reshape(row_count, HEADS * HEAD_DIM).astype(jnp.bfloat16)

def reference(queries, new_keys, new_values, key_cache, value_cache, lengths, out_weight, down_factors, up_factors, assignment, home_index):
    blocks = REQS // REQ_DEV

    def split_rows(array):
        return array.reshape((blocks, REQ_DEV) + array.shape[1:])
    pieces = (queries, new_keys, new_values, key_cache, value_cache, lengths)
    attended = lax.map(attend_block, tuple((split_rows(array) for array in pieces)))
    attended = attended.reshape(REQS, HEADS * HEAD_DIM)
    base = jnp.dot(attended, out_weight, preferred_element_type=jnp.float32)
    position = home_index[assignment]

    def add_variant(running, storage):
        selected = position == storage
        low_rank = jnp.dot(attended, down_factors[storage], preferred_element_type=jnp.float32).astype(jnp.bfloat16)
        delta_part = jnp.dot(low_rank, up_factors[storage], preferred_element_type=jnp.float32).astype(jnp.bfloat16)
        return (running + jnp.where(selected[:, None], delta_part.astype(jnp.float32), jnp.float32(0.0)), None)
    start_sum = jnp.zeros((REQS, DW), jnp.float32)
    delta_rows, _ = lax.scan(add_variant, start_sum, jnp.arange(VARIANTS, dtype=jnp.int32))
    return (base + delta_rows).astype(jnp.bfloat16)
```

```python
import functools
import math

import jax
import jax.numpy as jnp
from jax import lax
from jax.experimental import pallas as pl
from jax.experimental.pallas import tpu as pltpu
from jax.sharding import PartitionSpec as P

HEAD_DIM = 128
BLOCK = 16
VMEM_BYTES = 48 * 1024 * 1024


def row_index(assign_row, home_col, var_local, dp_count):
    rows = assign_row.shape[1]
    variants = home_col.shape[0]
    labels = lax.broadcasted_iota(jnp.int32, (variants, rows), 0)
    position = jnp.sum(
        jnp.where(labels == assign_row, home_col, 0).astype(jnp.float32), axis=0, keepdims=True
    )
    home = jnp.zeros((1, rows), jnp.int32)
    for d in range(1, dp_count):
        home = home + (position >= d * var_local - 0.5).astype(jnp.int32)
    padded = max(16, dp_count)
    same = lax.broadcasted_iota(jnp.int32, (padded, rows), 0) == home
    earlier = lax.broadcasted_iota(jnp.int32, (rows, rows), 0) < lax.broadcasted_iota(
        jnp.int32, (rows, rows), 1
    )
    before = jnp.dot(
        same.astype(jnp.float32).astype(jnp.bfloat16),
        earlier.astype(jnp.float32).astype(jnp.bfloat16),
        preferred_element_type=jnp.float32,
    )
    rank = jnp.sum(jnp.where(same, before, 0.0), axis=0, keepdims=True)
    return home, rank.astype(jnp.int32)


def column_index(assign_col, home_row, var_local, dp_count):
    rows = assign_col.shape[0]
    variants = home_row.shape[1]
    labels = lax.broadcasted_iota(jnp.int32, (rows, variants), 1)
    position = jnp.sum(
        jnp.where(labels == assign_col, home_row, 0).astype(jnp.float32), axis=1, keepdims=True
    )
    home = jnp.zeros((rows, 1), jnp.int32)
    for d in range(1, dp_count):
        home = home + (position >= d * var_local - 0.5).astype(jnp.int32)
    same = lax.broadcasted_iota(jnp.int32, (rows, 128), 1) == home
    earlier = lax.broadcasted_iota(jnp.int32, (rows, rows), 1) < lax.broadcasted_iota(
        jnp.int32, (rows, rows), 0
    )
    before = jnp.dot(
        earlier.astype(jnp.float32).astype(jnp.bfloat16),
        same.astype(jnp.float32).astype(jnp.bfloat16),
        preferred_element_type=jnp.float32,
    )
    rank = jnp.sum(jnp.where(same, before, 0.0), axis=1, keepdims=True)
    return position.astype(jnp.int32), home, rank.astype(jnp.int32)


def attend_kernel(
    heads, kv_local, cache_len, var_local, dp_count, slots,
    info_ref, q_ref, nk_ref, nv_ref, k_ref, v_ref, assign_ref, home_ref, *rest
):
    att_ref = rest[0]
    slot_refs = rest[1 : 1 + dp_count]
    q_scr, o_scr = rest[1 + dp_count :]
    step = pl.program_id(0)
    group = heads // kv_local
    scale = 1.0 / math.sqrt(HEAD_DIM)
    q = q_ref[...].astype(jnp.float32) * scale
    for h in range(heads):
        q_scr[pl.ds(h, BLOCK, stride=heads), :] = q[:, h * HEAD_DIM : (h + 1) * HEAD_DIM]
    total = BLOCK * heads
    head = lax.broadcasted_iota(jnp.int32, (total, 1), 0) % heads
    q_all = q_scr[...]
    parts = [
        jnp.where((head >= k * group) & (head < (k + 1) * group), q_all, 0.0)
        for k in range(kv_local)
    ]
    q_bd = (parts[0] if kv_local == 1 else jnp.concatenate(parts, axis=1)).astype(jnp.bfloat16)
    nt = (((1,), (1,)), ((), ()))
    own_all = lax.dot_general(q_bd, nk_ref[...], nt, preferred_element_type=jnp.float32)
    own_req = lax.broadcasted_iota(jnp.int32, (total, BLOCK), 0) // heads
    own_valid = own_req == lax.broadcasted_iota(jnp.int32, (total, BLOCK), 1)
    own_all = jnp.where(own_valid, own_all, -1e30)
    wide = 2 * cache_len
    tall = 2 * heads
    row = lax.broadcasted_iota(jnp.int32, (tall, wide), 0)
    lane = lax.broadcasted_iota(jnp.int32, (tall, wide), 1)
    first = row < heads
    lane_in = lane - jnp.where(first, 0, cache_len)
    for p in range(BLOCK // 2):
        keys = k_ref[2 * p : 2 * p + 2].reshape(wide, kv_local * HEAD_DIM)
        values = v_ref[2 * p : 2 * p + 2].reshape(wide, kv_local * HEAD_DIM)
        scores = lax.dot_general(
            q_bd[p * tall : (p + 1) * tall], keys, nt, preferred_element_type=jnp.float32
        )
        len_a = info_ref[1 + step * BLOCK + 2 * p]
        len_b = info_ref[1 + step * BLOCK + 2 * p + 1]
        valid = (lane_in >= 0) & (lane_in < jnp.where(first, jnp.minimum(len_a, cache_len), len_b))
        scores = jnp.where(valid, scores, -1e30)
        own = own_all[p * tall : (p + 1) * tall]
        highest = jnp.maximum(
            jnp.max(scores, axis=1, keepdims=True), jnp.max(own, axis=1, keepdims=True)
        )
        weights = jnp.exp(scores - highest)
        own_weights = jnp.exp(own - highest)
        denominator = jnp.sum(weights, axis=1, keepdims=True) + jnp.sum(
            own_weights, axis=1, keepdims=True
        )
        result = jnp.dot(
            weights.astype(jnp.bfloat16), values, preferred_element_type=jnp.float32
        ) + jnp.dot(
            own_weights.astype(jnp.bfloat16), nv_ref[...], preferred_element_type=jnp.float32
        )
        result = result * (1.0 / denominator)
        picked = result[:, :HEAD_DIM]
        for k in range(1, kv_local):
            picked = jnp.where(
                head[:tall] >= k * group, result[:, k * HEAD_DIM : (k + 1) * HEAD_DIM], picked
            )
        o_scr[p * tall : (p + 1) * tall, :] = picked
    where = pl.ds(pl.multiple_of(step * BLOCK, BLOCK), BLOCK)
    for h in range(heads):
        att_ref[where, h * HEAD_DIM : (h + 1) * HEAD_DIM] = o_scr[
            pl.ds(h, BLOCK, stride=heads), :
        ].astype(jnp.bfloat16)

    @pl.when(step == pl.num_programs(0) - 1)
    def _():
        rows = att_ref.shape[0]
        home, rank = row_index(assign_ref[...], home_ref[...], var_local, dp_count)
        slot = lax.broadcasted_iota(jnp.int32, (slots, rows), 0)
        attended = att_ref[...]
        for shift in range(dp_count):
            target = lax.rem(info_ref[0] + shift, dp_count)
            pick = (slot == rank) & (home == target)
            slot_refs[shift][...] = jnp.dot(
                pick.astype(jnp.float32).astype(jnp.bfloat16),
                attended,
                preferred_element_type=jnp.float32,
            ).astype(jnp.bfloat16)


def attend(
    info, queries, new_keys, new_values, key_cache, value_cache, assign_row, home_col,
    var_local, dp_count, slots,
):
    rows, width = queries.shape
    kv_width = new_keys.shape[1]
    cache_len = key_cache.shape[1]
    heads, kv_local = width // HEAD_DIM, kv_width // HEAD_DIM
    spec = pltpu.PrefetchScalarGridSpec(
        num_scalar_prefetch=1,
        grid=(rows // BLOCK,),
        in_specs=[
            pl.BlockSpec((BLOCK, width), lambda i, _: (i, 0)),
            pl.BlockSpec((BLOCK, kv_width), lambda i, _: (i, 0)),
            pl.BlockSpec((BLOCK, kv_width), lambda i, _: (i, 0)),
            pl.BlockSpec((BLOCK, cache_len, kv_width), lambda i, _: (i, 0, 0)),
            pl.BlockSpec((BLOCK, cache_len, kv_width), lambda i, _: (i, 0, 0)),
            pl.BlockSpec(assign_row.shape, lambda i, _: (0, 0)),
            pl.BlockSpec(home_col.shape, lambda i, _: (0, 0)),
        ],
        out_specs=[pl.BlockSpec((rows, width), lambda i, _: (0, 0))]
        + [pl.BlockSpec((slots, width), lambda i, _: (0, 0))] * dp_count,
        scratch_shapes=[
            pltpu.VMEM((BLOCK * heads, HEAD_DIM), jnp.float32),
            pltpu.VMEM((BLOCK * heads, HEAD_DIM), jnp.float32),
        ],
    )
    return pl.pallas_call(
        functools.partial(
            attend_kernel, heads, kv_local, cache_len, var_local, dp_count, slots
        ),
        grid_spec=spec,
        out_shape=[jax.ShapeDtypeStruct((rows, width), jnp.bfloat16)]
        + [jax.ShapeDtypeStruct((slots, width), jnp.bfloat16)] * dp_count,
        compiler_params=pltpu.CompilerParams(vmem_limit_bytes=VMEM_BYTES),
        name="attend",
    )(info, queries, new_keys, new_values, key_cache, value_cache, assign_row, home_col)


def project_kernel(ids_ref, a_ref, *refs):
    count = len(refs) // 2
    for w_ref, o_ref in zip(refs[:count], refs[count:]):
        o_ref[...] = jnp.dot(
            a_ref[...], w_ref[...], preferred_element_type=jnp.float32
        ).astype(jnp.bfloat16)


def project(ids, attended, out_weight, which, out_local):
    rows, width = attended.shape
    tile = min(256, out_local)
    tiles = out_local // tile

    def column(w):
        return lambda i, ids: (0, ids[w] * tiles + i)

    spec = pltpu.PrefetchScalarGridSpec(
        num_scalar_prefetch=1,
        grid=(tiles,),
        in_specs=[pl.BlockSpec((rows, width), lambda i, _: (0, 0))]
        + [pl.BlockSpec((width, tile), column(w)) for w in which],
        out_specs=[pl.BlockSpec((rows, tile), lambda i, _: (0, i)) for _ in which],
    )
    return pl.pallas_call(
        project_kernel,
        grid_spec=spec,
        out_shape=[jax.ShapeDtypeStruct((rows, out_local), jnp.bfloat16) for _ in which],
        compiler_params=pltpu.CompilerParams(vmem_limit_bytes=VMEM_BYTES),
        name="project",
    )(ids, attended, *([out_weight] * len(which)))


def reduce_kernel(rows_ref, down_ref, o_ref):
    for v in range(down_ref.shape[0]):
        o_ref[v] = jnp.dot(
            rows_ref[...], down_ref[v], preferred_element_type=jnp.float32
        ).astype(o_ref.dtype)


def reduce_rows(rows, down):
    return pl.pallas_call(
        reduce_kernel,
        out_shape=jax.ShapeDtypeStruct((down.shape[0], rows.shape[0], down.shape[2]), jnp.bfloat16),
        compiler_params=pltpu.CompilerParams(vmem_limit_bytes=VMEM_BYTES),
        name="reduce_rows",
    )(rows, down)


def combine_kernel(var_local, dp_count, info_ref, assign_ref, home_ref, *refs):
    o_ref = refs[-1]
    position, home, rank = column_index(assign_ref[...], home_ref[...], var_local, dp_count)
    local = position - home * var_local
    rows = assign_ref.shape[0]
    slots = refs[0].shape[1]
    slot = lax.broadcasted_iota(jnp.int32, (rows, slots), 1)
    total = jnp.zeros(o_ref.shape, jnp.float32)
    for shift in range(dp_count):
        target = lax.rem(info_ref[0] + shift, dp_count)
        mine = (slot == rank) & (home == target)
        for v in range(var_local):
            pick = (mine & (local == v)).astype(jnp.float32).astype(jnp.bfloat16)
            total = total + jnp.dot(pick, refs[shift][v], preferred_element_type=jnp.float32)
    o_ref[...] = total


def combine(info, assign_col, home_row, parts, var_local, dp_count):
    rows = assign_col.shape[0]
    rank_width = parts[0].shape[2]
    vmem = pl.BlockSpec(memory_space=pltpu.VMEM)
    return pl.pallas_call(
        functools.partial(combine_kernel, var_local, dp_count),
        in_specs=[pl.BlockSpec(memory_space=pltpu.SMEM)] + [vmem] * (2 + len(parts)),
        out_specs=vmem,
        out_shape=jax.ShapeDtypeStruct((rows, rank_width), jnp.float32),
        compiler_params=pltpu.CompilerParams(vmem_limit_bytes=VMEM_BYTES),
        name="combine",
    )(info, assign_col, home_row, *parts)


def delta_kernel(
    var_local, dp_count, info_ref, assign_ref, home_ref, low_ref, base_ref, up_ref, *refs
):
    o_ref = refs[-1]
    position, home, _ = column_index(assign_ref[...], home_ref[...], var_local, dp_count)
    low = low_ref[...].astype(jnp.bfloat16)
    rows = low.shape[0]
    half = refs[0].shape[2]

    def picked(target, v):
        return jnp.where(position == target * var_local + v, low.astype(jnp.float32), 0.0).astype(
            jnp.bfloat16
        )

    own = [picked(info_ref[0], v) for v in range(var_local)]
    others = [
        [picked(lax.rem(info_ref[0] + dp_count - shift, dp_count), v) for v in range(var_local)]
        for shift in range(1, dp_count)
    ]
    for side in range(2):
        place = lax.rem(info_ref[1] + side, 2)
        columns = pl.ds(pl.multiple_of(place * half, half), half)
        total = jnp.zeros((rows, half), jnp.float32)
        for v in range(var_local):
            total = total + jnp.dot(own[v], up_ref[v, :, columns], preferred_element_type=jnp.float32)
            for shift in range(1, dp_count):
                total = total + jnp.dot(
                    others[shift - 1][v],
                    refs[side * (dp_count - 1) + shift - 1][v],
                    preferred_element_type=jnp.float32,
                )
        o_ref[:, columns] = (base_ref[:, columns].astype(jnp.float32) + total).astype(jnp.bfloat16)


def add_delta(info, assign_col, home_row, low, base, up, near, far, var_local, dp_count):
    vmem = pl.BlockSpec(memory_space=pltpu.VMEM)
    return pl.pallas_call(
        functools.partial(delta_kernel, var_local, dp_count),
        in_specs=[pl.BlockSpec(memory_space=pltpu.SMEM)] + [vmem] * (5 + len(near) + len(far)),
        out_specs=vmem,
        out_shape=jax.ShapeDtypeStruct(base.shape, jnp.bfloat16),
        compiler_params=pltpu.CompilerParams(vmem_limit_bytes=VMEM_BYTES),
        name="add_delta",
    )(info, assign_col, home_row, low, base, up, *near, *far)


def per_device(
    queries, new_keys, new_values, key_cache, value_cache, lengths,
    out_weight, down_factors, up_factors, assignment, home_index,
):
    dp_count = lax.axis_size("dp")
    tensor_count = lax.axis_size("tensor")
    group_count = lax.axis_size("groups")
    z = lax.axis_index("dp").astype(jnp.int32)
    t = lax.axis_index("tensor").astype(jnp.int32)
    y = lax.axis_index("groups").astype(jnp.int32)
    rows = queries.shape[0]
    var_local = down_factors.shape[0]
    variants = var_local * dp_count
    out_local = up_factors.shape[2]
    capacity = max(2, 5 * rows // (2 * variants))
    slots = min(rows, -(-var_local * capacity // 16) * 16)
    bits = tensor_count.bit_length() - 1

    def along(values, axis, count, shift):
        return lax.ppermute(values, axis, [(i, (i + shift) % count) for i in range(count)])

    def across(values, bit):
        return lax.ppermute(
            values, "tensor", [(i, i ^ (1 << bit)) for i in range(tensor_count)]
        )

    half = out_local // 2
    piece = lax.dynamic_slice_in_dim(up_factors, y * half, half, axis=2)
    near, far = [], []
    for shift in range(1, dp_count):
        piece = along(piece, "dp", dp_count, 1)
        near.append(piece)
        far.append(along(piece, "groups", group_count, 1))

    assign_row, assign_col = assignment[None, :], assignment[:, None]
    home_row, home_col = home_index[None, :], home_index[:, None]
    place = jnp.stack([z, y])
    attended, *outgoing = attend(
        jnp.concatenate([z[None], lengths]), queries, new_keys, new_values, key_cache, value_cache,
        assign_row, home_col, var_local, dp_count, slots,
    )
    arrived = [outgoing[0]] + [
        along(outgoing[shift], "dp", dp_count, shift) for shift in range(1, dp_count)
    ]

    ids = t ^ jnp.arange(tensor_count, dtype=jnp.int32)
    held = {}
    order = [w for w in range(tensor_count) if w & 1] + [
        w for w in range(tensor_count) if not w & 1
    ]
    middle = tensor_count // 2
    for which in (order[:middle], order[middle:]):
        for w, product in zip(which, project(ids, attended, out_weight, which, out_local)):
            held[w] = product
    for bit in range(bits):
        kept = {}
        for w in list(held):
            if w & (1 << bit):
                continue
            got = across(held[w | (1 << bit)], bit)
            kept[w] = held[w].astype(jnp.float32) + got.astype(jnp.float32)
            if bit < bits - 1 and w:
                kept[w] = kept[w].astype(jnp.bfloat16)
        held = kept
    base = held[0]

    returned = []
    for shift in range(dp_count):
        part = reduce_rows(arrived[shift], down_factors)
        returned.append(part if shift == 0 else along(part, "dp", dp_count, dp_count - shift))
    low = combine(place, assign_col, home_row, returned, var_local, dp_count)
    for bit in range(bits):
        low = low + across(low, bit)
    mixed = add_delta(
        place, assign_col, home_row, low, base, up_factors, near, far, var_local, dp_count
    )

    pieces = {0: mixed}
    for bit in reversed(range(bits)):
        for w in list(pieces):
            pieces[w | (1 << bit)] = across(pieces[w], bit)
    whole = jnp.zeros((rows, tensor_count * out_local), jnp.bfloat16)
    for w, value in pieces.items():
        whole = lax.dynamic_update_slice(whole, value, (jnp.int32(0), (t ^ w) * out_local))
    return whole


def solution(mesh):
    placed = (
        P(("groups", "dp"), "tensor"),
        P(("groups", "dp"), "tensor"),
        P(("groups", "dp"), "tensor"),
        P(("groups", "dp"), None, "tensor"),
        P(("groups", "dp"), None, "tensor"),
        P(("groups", "dp")),
        P("tensor", None),
        P("dp", "tensor", None),
        P("dp", None, "tensor"),
        P(("groups", "dp")),
        P(),
    )
    return jax.shard_map(
        per_device, mesh=mesh, in_specs=placed, out_specs=P(("groups", "dp"), None), check_vma=False
    )
```

```python
import functools
import math

import jax
import jax.numpy as jnp
from jax import lax
from jax.experimental import pallas as pl
from jax.experimental.pallas import tpu as pltpu
from jax.sharding import PartitionSpec as P

HEAD_DIM = 128
BLOCK = 32
FREE = pl.CostEstimate(flops=0, bytes_accessed=0, transcendentals=0)
NT = (((1,), (1,)), ((), ()))


def params(mebibytes):
    return pltpu.CompilerParams(vmem_limit_bytes=mebibytes * 1024 * 1024)


def one_hot(mask):
    return mask.astype(jnp.float32).astype(jnp.bfloat16)


def iota(shape, axis):
    return lax.broadcasted_iota(jnp.int32, shape, axis)


def index_row(assign_row, home_ref, var_local, dp_count):
    rows = assign_row.shape[1]
    position = jnp.zeros((1, rows), jnp.int32)
    for v in range(var_local * dp_count):
        position = jnp.where(assign_row == v, home_ref[v], position)
    home = jnp.zeros((1, rows), jnp.int32)
    for d in range(1, dp_count):
        home = home + (position >= d * var_local).astype(jnp.int32)
    same = iota((max(16, dp_count), rows), 0) == home
    earlier = iota((rows, rows), 0) < iota((rows, rows), 1)
    before = jnp.dot(one_hot(same), one_hot(earlier), preferred_element_type=jnp.float32)
    rank = jnp.sum(jnp.where(same, before, 0.0), axis=0, keepdims=True)
    return position, home, rank.astype(jnp.int32)


def as_column(row):
    rows = row.shape[1]
    spread = jnp.where(iota((rows, rows), 0) == iota((rows, rows), 1), row.astype(jnp.float32), 0.0)
    return jnp.sum(spread, axis=1, keepdims=True).astype(jnp.int32)


def attend_kernel(
    var_local, dp_count, slots,
    q_hbm, nk_hbm, nv_hbm, k_hbm, v_hbm, len_hbm, assign_hbm, home_hbm, *rest
):
    att_ref = rest[0]
    slot_refs = rest[1 : 1 + dp_count]
    (q_buf, nk_buf, nv_buf, k_buf, v_buf, len_ref, assign_ref, home_ref, q_scr, o_scr,
     small_sem, k_sem, v_sem) = rest[1 + dp_count :]
    rows, width = q_buf.shape
    cache_len = k_buf.shape[1]
    heads, kv_local = width // HEAD_DIM, nk_buf.shape[1] // HEAD_DIM
    group = heads // kv_local
    blocks = rows // BLOCK
    scale = 1.0 / math.sqrt(HEAD_DIM)
    small = [
        pltpu.make_async_copy(source, target, small_sem.at[i])
        for i, (source, target) in enumerate((
            (q_hbm, q_buf), (nk_hbm, nk_buf), (nv_hbm, nv_buf), (len_hbm, len_ref),
            (assign_hbm, assign_ref), (home_hbm, home_ref),
        ))
    ]

    def cached(i):
        at = pl.ds(i * BLOCK, BLOCK)
        return (
            pltpu.make_async_copy(k_hbm.at[at], k_buf.at[at], k_sem.at[i]),
            pltpu.make_async_copy(v_hbm.at[at], v_buf.at[at], v_sem.at[i]),
        )

    for copy in small:
        copy.start()
    for i in range(blocks):
        for copy in cached(i):
            copy.start()
    for copy in small:
        copy.wait()
    total = BLOCK * heads
    head = iota((total, 1), 0) % heads
    own_valid = iota((total, BLOCK), 0) // heads == iota((total, BLOCK), 1)
    lane = iota((heads, cache_len), 1)

    def block(step, carry):
        at = pl.ds(pl.multiple_of(step * BLOCK, BLOCK), BLOCK)
        q = q_buf[at, :].astype(jnp.float32)
        for h in range(heads):
            q_scr[pl.ds(h, BLOCK, stride=heads), :] = q[:, h * HEAD_DIM : (h + 1) * HEAD_DIM]
        q_all = q_scr[...]
        parts = [
            jnp.where((head >= k * group) & (head < (k + 1) * group), q_all, 0.0)
            for k in range(kv_local)
        ]
        q_bd = (parts[0] if kv_local == 1 else jnp.concatenate(parts, axis=1)).astype(jnp.bfloat16)
        own = lax.dot_general(q_bd, nk_buf[at, :], NT, preferred_element_type=jnp.float32)
        own = jnp.where(own_valid, own * scale, -1e30)
        key_copy, value_copy = cached(step)
        key_copy.wait()
        scores = jnp.concatenate(
            [
                jnp.where(
                    lane < len_ref[step * BLOCK + r],
                    lax.dot_general(
                        q_bd[r * heads : (r + 1) * heads],
                        k_buf[step * BLOCK + r],
                        NT,
                        preferred_element_type=jnp.float32,
                    )
                    * scale,
                    -1e30,
                )
                for r in range(BLOCK)
            ],
            axis=0,
        )
        highest = jnp.maximum(
            jnp.max(scores, axis=1, keepdims=True), jnp.max(own, axis=1, keepdims=True)
        )
        weights = jnp.exp(scores - highest)
        own_weights = jnp.exp(own - highest)
        inverse = 1.0 / (
            jnp.sum(weights, axis=1, keepdims=True) + jnp.sum(own_weights, axis=1, keepdims=True)
        )
        weights = (weights * inverse).astype(jnp.bfloat16)
        own_weights = (own_weights * inverse).astype(jnp.bfloat16)
        own_result = jnp.dot(own_weights, nv_buf[at, :], preferred_element_type=jnp.float32)
        value_copy.wait()
        for r in range(BLOCK):
            mine = slice(r * heads, (r + 1) * heads)
            result = own_result[mine] + jnp.dot(
                weights[mine], v_buf[step * BLOCK + r], preferred_element_type=jnp.float32
            )
            picked = result[:, :HEAD_DIM]
            for k in range(1, kv_local):
                picked = jnp.where(
                    head[:heads] >= k * group, result[:, k * HEAD_DIM : (k + 1) * HEAD_DIM], picked
                )
            o_scr[mine, :] = picked
        for h in range(heads):
            att_ref[at, h * HEAD_DIM : (h + 1) * HEAD_DIM] = o_scr[
                pl.ds(h, BLOCK, stride=heads), :
            ].astype(jnp.bfloat16)
        return carry

    lax.fori_loop(0, blocks, block, 0)
    _, home, rank = index_row(assign_ref[...], home_ref, var_local, dp_count)
    slot = iota((slots, rows), 0)
    attended = att_ref[...]
    for shift in range(dp_count):
        pick = (slot == rank) & (home == lax.rem(lax.axis_index("dp") + shift, dp_count))
        slot_refs[shift][...] = jnp.dot(
            one_hot(pick), attended, preferred_element_type=jnp.float32
        ).astype(jnp.bfloat16)


def attend(
    queries, new_keys, new_values, key_cache, value_cache, lengths, assign_row, home_index,
    var_local, dp_count, slots,
):
    rows, width = queries.shape
    heads = width // HEAD_DIM
    blocks = rows // BLOCK
    vmem = pl.BlockSpec(memory_space=pltpu.VMEM)
    given = (queries, new_keys, new_values, key_cache, value_cache)
    return pl.pallas_call(
        functools.partial(attend_kernel, var_local, dp_count, slots),
        in_specs=[pl.BlockSpec(memory_space=pltpu.HBM)] * 8,
        out_specs=[vmem] * (1 + dp_count),
        out_shape=[jax.ShapeDtypeStruct((rows, width), jnp.bfloat16)]
        + [jax.ShapeDtypeStruct((slots, width), jnp.bfloat16)] * dp_count,
        scratch_shapes=[pltpu.VMEM(a.shape, a.dtype) for a in given]
        + [
            pltpu.SMEM(lengths.shape, jnp.int32),
            pltpu.VMEM(assign_row.shape, jnp.int32),
            pltpu.SMEM(home_index.shape, jnp.int32),
            pltpu.VMEM((BLOCK * heads, HEAD_DIM), jnp.float32),
            pltpu.VMEM((BLOCK * heads, HEAD_DIM), jnp.float32),
            pltpu.SemaphoreType.DMA((6,)),
            pltpu.SemaphoreType.DMA((blocks,)),
            pltpu.SemaphoreType.DMA((blocks,)),
        ],
        compiler_params=params(61),
        cost_estimate=FREE,
        name="attend",
    )(*given, lengths, assign_row, home_index)


def project_kernel(count, a_ref, w_hbm, *rest):
    outs, (w_buf, sem) = rest[:count], rest[count:]
    width = w_buf.shape[2]
    out_local = outs[0].shape[1]
    per = out_local // width
    me = lax.axis_index("tensor")
    order = [w for w in range(count) if w & 1] + [w for w in range(count) if not w & 1]

    def fetch(n):
        column = ((me ^ order[n // per]) * per + n % per) * width
        return pltpu.make_async_copy(
            w_hbm.at[:, pl.ds(pl.multiple_of(column, width), width)], w_buf.at[n], sem.at[n]
        )

    for n in range(count * per):
        fetch(n).start()
    attended = a_ref[...]
    for n in range(count * per):
        fetch(n).wait()
        at = slice(n % per * width, (n % per + 1) * width)
        outs[order[n // per]][:, at] = jnp.dot(
            attended, w_buf[n], preferred_element_type=jnp.float32
        ).astype(jnp.bfloat16)


def project(attended, out_weight, count, out_local):
    rows, depth = attended.shape
    width = min(512, out_local)
    tiles = out_weight.shape[1] // width
    vmem = pl.BlockSpec(memory_space=pltpu.VMEM)
    return pl.pallas_call(
        functools.partial(project_kernel, count),
        in_specs=[vmem, pl.BlockSpec(memory_space=pltpu.HBM)],
        out_specs=[vmem] * count,
        out_shape=[jax.ShapeDtypeStruct((rows, out_local), jnp.bfloat16)] * count,
        scratch_shapes=[
            pltpu.VMEM((tiles, depth, width), jnp.bfloat16),
            pltpu.SemaphoreType.DMA((tiles,)),
        ],
        compiler_params=params(44),
        cost_estimate=FREE,
        name="project",
    )(attended, out_weight)


def reduce_kernel(rows_ref, down_ref, o_ref):
    o_ref[...] = lax.dot_general(
        rows_ref[...], down_ref[...], NT, preferred_element_type=jnp.float32
    ).astype(o_ref.dtype)


def reduce_rows(rows, down):
    return pl.pallas_call(
        reduce_kernel,
        out_shape=jax.ShapeDtypeStruct((rows.shape[0], down.shape[0]), jnp.bfloat16),
        compiler_params=params(8),
        cost_estimate=FREE,
        name="reduce_rows",
    )(rows, down)


def combine_kernel(var_local, dp_count, assign_ref, home_ref, *refs):
    o_ref = refs[-1]
    index = index_row(assign_ref[...], home_ref, var_local, dp_count)
    position, home, rank = [as_column(part) for part in index]
    rows, rank_width = o_ref.shape
    slots, wide = refs[0].shape
    slot = iota((rows, slots), 1)
    total = jnp.zeros((rows, wide), jnp.float32)
    for shift in range(dp_count):
        pick = (slot == rank) & (home == lax.rem(lax.axis_index("dp") + shift, dp_count))
        total = total + jnp.dot(one_hot(pick), refs[shift][...], preferred_element_type=jnp.float32)
    local = position - home * var_local
    start = local * rank_width
    lane = iota((rows, wide), 1)
    total = jnp.where((lane >= start) & (lane < start + rank_width), total, 0.0)
    low = total[:, :rank_width]
    for v in range(1, var_local):
        low = low + total[:, v * rank_width : (v + 1) * rank_width]
    o_ref[...] = low


def combine(assign_row, home_index, parts, rank_width, var_local, dp_count):
    vmem = pl.BlockSpec(memory_space=pltpu.VMEM)
    return pl.pallas_call(
        functools.partial(combine_kernel, var_local, dp_count),
        in_specs=[vmem, pl.BlockSpec(memory_space=pltpu.SMEM)] + [vmem] * len(parts),
        out_specs=vmem,
        out_shape=jax.ShapeDtypeStruct((assign_row.shape[1], rank_width), jnp.float32),
        compiler_params=params(8),
        cost_estimate=FREE,
        name="combine",
    )(assign_row, home_index, *parts)


def delta_kernel(var_local, dp_count, assign_ref, home_ref, low_ref, got_ref, base_ref, add_ref, up_ref, *refs):
    o_ref = refs[-1]
    index = index_row(assign_ref[...], home_ref, var_local, dp_count)
    position = as_column(index[0])
    low = (low_ref[...] + got_ref[...]).astype(jnp.bfloat16)
    rows, rank_width = low.shape
    half = refs[0].shape[1]
    wide = up_ref.shape[0]
    spread = one_hot(iota((rank_width, wide), 1) % rank_width == iota((rank_width, wide), 0))
    low = jnp.dot(low, spread, preferred_element_type=jnp.float32)
    factor = iota((rows, wide), 1) // rank_width
    me = lax.axis_index("dp")

    def picked(shift):
        target = lax.rem(me + dp_count - shift, dp_count)
        return jnp.where(position == target * var_local + factor, low, 0.0).astype(jnp.bfloat16)

    mine = [picked(shift) for shift in range(dp_count)]
    for side in range(2):
        place = lax.rem(lax.axis_index("groups") + side, 2)
        columns = pl.ds(pl.multiple_of(place * half, half), half)
        total = jnp.dot(mine[0], up_ref[:, columns], preferred_element_type=jnp.float32)
        for shift in range(1, dp_count):
            total = total + jnp.dot(
                mine[shift],
                refs[side * (dp_count - 1) + shift - 1][...],
                preferred_element_type=jnp.float32,
            )
        base = base_ref[:, columns].astype(jnp.float32) + add_ref[:, columns].astype(jnp.float32)
        o_ref[:, columns] = (base + total).astype(jnp.bfloat16)


def add_delta(assign_row, home_index, low, got, base, add, up, near, far, var_local, dp_count):
    vmem = pl.BlockSpec(memory_space=pltpu.VMEM)
    return pl.pallas_call(
        functools.partial(delta_kernel, var_local, dp_count),
        in_specs=[vmem, pl.BlockSpec(memory_space=pltpu.SMEM)] + [vmem] * (5 + len(near) + len(far)),
        out_specs=vmem,
        out_shape=jax.ShapeDtypeStruct(base.shape, jnp.bfloat16),
        compiler_params=params(16),
        cost_estimate=FREE,
        name="add_delta",
    )(assign_row, home_index, low, got, base, add, up, *near, *far)


def per_device(
    queries, new_keys, new_values, key_cache, value_cache, lengths,
    out_weight, down_factors, up_factors, assignment, home_index,
):
    dp_count = lax.axis_size("dp")
    tensor_count = lax.axis_size("tensor")
    group_count = lax.axis_size("groups")
    t = lax.axis_index("tensor").astype(jnp.int32)
    y = lax.axis_index("groups").astype(jnp.int32)
    rows = queries.shape[0]
    var_local, _, rank_width = down_factors.shape
    variants = var_local * dp_count
    out_local = up_factors.shape[2]
    capacity = max(2, 5 * rows // (2 * variants))
    slots = min(rows, -(-var_local * capacity // 16) * 16)
    bits = tensor_count.bit_length() - 1

    def along(values, axis, count, shift):
        return lax.ppermute(values, axis, [(i, (i + shift) % count) for i in range(count)])

    def across(values, bit):
        return lax.ppermute(
            values, "tensor", [(i, i ^ (1 << bit)) for i in range(tensor_count)]
        )

    half = out_local // 2
    up = up_factors.reshape(var_local * rank_width, out_local)
    piece = lax.dynamic_slice_in_dim(up, y * half, half, axis=1)
    near, far = [], []
    for _ in range(1, dp_count):
        piece = along(piece, "dp", dp_count, 1)
        near.append(piece)
        far.append(along(piece, "groups", group_count, 1))

    assign_row = assignment[None, :]
    attended, *outgoing = attend(
        queries, new_keys, new_values, key_cache, value_cache, lengths, assign_row, home_index,
        var_local, dp_count, slots,
    )
    arrived = [outgoing[0]] + [
        along(outgoing[shift], "dp", dp_count, shift) for shift in range(1, dp_count)
    ]

    held = dict(enumerate(project(attended, out_weight, tensor_count, out_local)))
    for bit in range(bits):
        kept = {}
        for w in list(held):
            if w & (1 << bit):
                continue
            got = across(held[w | (1 << bit)], bit)
            if bit == bits - 1:
                add = got
                kept[w] = held[w]
            else:
                kept[w] = held[w].astype(jnp.float32) + got.astype(jnp.float32)
                if w:
                    kept[w] = kept[w].astype(jnp.bfloat16)
        held = kept

    down = jnp.swapaxes(down_factors, 1, 2).reshape(var_local * rank_width, -1)
    returned = []
    for shift in range(dp_count):
        part = reduce_rows(arrived[shift], down)
        returned.append(part if shift == 0 else along(part, "dp", dp_count, dp_count - shift))
    low = combine(assign_row, home_index, returned, rank_width, var_local, dp_count)
    for bit in range(bits - 1):
        low = low + across(low, bit)
    low_got = across(low, bits - 1)
    mixed = add_delta(
        assign_row, home_index, low, low_got, held[0], add, up, near, far, var_local, dp_count
    )

    pieces = {0: mixed}
    for bit in reversed(range(bits)):
        for w in list(pieces):
            pieces[w | (1 << bit)] = across(pieces[w], bit)
    whole = jnp.zeros((rows, tensor_count * out_local), jnp.bfloat16)
    for w, value in pieces.items():
        whole = lax.dynamic_update_slice(whole, value, (jnp.int32(0), (t ^ w) * out_local))
    return whole


def solution(mesh):
    placed = (
        P(("groups", "dp"), "tensor"),
        P(("groups", "dp"), "tensor"),
        P(("groups", "dp"), "tensor"),
        P(("groups", "dp"), None, "tensor"),
        P(("groups", "dp"), None, "tensor"),
        P(("groups", "dp")),
        P("tensor", None),
        P("dp", "tensor", None),
        P("dp", None, "tensor"),
        P(("groups", "dp")),
        P(),
    )
    return jax.shard_map(
        per_device, mesh=mesh, in_specs=placed, out_specs=P(("groups", "dp"), None), check_vma=False
    )
```

```python
import functools
import math

import jax
import jax.numpy as jnp
from jax import lax
from jax.experimental import pallas as pl
from jax.experimental.pallas import tpu as pltpu
from jax.sharding import PartitionSpec as P

HEAD_DIM = 128
BLOCK = 32
FLAG = 64
FREE = pl.CostEstimate(flops=0, bytes_accessed=0, transcendentals=0)
NT = (((1,), (1,)), ((), ()))


def params(mebibytes):
    return pltpu.CompilerParams(vmem_limit_bytes=mebibytes * 1024 * 1024)


def one_hot(mask):
    return mask.astype(jnp.float32).astype(jnp.bfloat16)


def iota(shape, axis):
    return lax.broadcasted_iota(jnp.int32, shape, axis)


def index_row(assign_row, home_ref, var_local, dp_count):
    rows = assign_row.shape[1]
    position = jnp.zeros((1, rows), jnp.int32)
    for v in range(var_local * dp_count):
        position = jnp.where(assign_row == v, home_ref[v], position)
    home = jnp.zeros((1, rows), jnp.int32)
    for d in range(1, dp_count):
        home = home + (position >= d * var_local).astype(jnp.int32)
    same = iota((max(16, dp_count), rows), 0) == home
    earlier = iota((rows, rows), 0) < iota((rows, rows), 1)
    before = jnp.dot(one_hot(same), one_hot(earlier), preferred_element_type=jnp.float32)
    rank = jnp.sum(jnp.where(same, before, 0.0), axis=0, keepdims=True)
    return position, home, rank.astype(jnp.int32)


def as_column(row):
    rows = row.shape[1]
    spread = jnp.where(iota((rows, rows), 0) == iota((rows, rows), 1), row.astype(jnp.float32), 0.0)
    return jnp.sum(spread, axis=1, keepdims=True).astype(jnp.int32)


def gate(mebibytes, values, ties):
    hbm = pl.BlockSpec(memory_space=pl.ANY)
    count = len(values)
    return pl.pallas_call(
        lambda *refs: None,
        in_specs=[hbm] * (count + len(ties)),
        out_specs=[hbm] * count,
        out_shape=[jax.ShapeDtypeStruct(v.shape, v.dtype) for v in values],
        input_output_aliases={i: i for i in range(count)},
        compiler_params=params(mebibytes),
        cost_estimate=FREE,
        name="gate",
    )(*values, *ties)


def attend_kernel(
    var_local, dp_count,
    q_hbm, nk_hbm, nv_hbm, k_hbm, v_hbm, len_hbm, assign_hbm, home_hbm, *rest
):
    att_ref = rest[0]
    slot_refs = rest[1 : 1 + dp_count]
    flag_ref = rest[1 + dp_count]
    (q_buf, nk_buf, nv_buf, k_buf, v_buf, len_ref, assign_ref, home_ref, q_scr, o_scr,
     small_sem, k_sem, v_sem) = rest[2 + dp_count :]
    rows, width = q_buf.shape
    cache_len = k_buf.shape[1]
    heads, kv_local = width // HEAD_DIM, nk_buf.shape[1] // HEAD_DIM
    group = heads // kv_local
    blocks = rows // BLOCK
    scale = 1.0 / math.sqrt(HEAD_DIM)
    small = [
        pltpu.make_async_copy(source, target, small_sem.at[i])
        for i, (source, target) in enumerate((
            (q_hbm, q_buf), (nk_hbm, nk_buf), (nv_hbm, nv_buf), (len_hbm, len_ref),
            (assign_hbm, assign_ref), (home_hbm, home_ref),
        ))
    ]

    def cached(i):
        at = pl.ds(i * BLOCK, BLOCK)
        return (
            pltpu.make_async_copy(k_hbm.at[at], k_buf.at[at], k_sem.at[i]),
            pltpu.make_async_copy(v_hbm.at[at], v_buf.at[at], v_sem.at[i]),
        )

    for copy in small:
        copy.start()
    for i in range(blocks):
        for copy in cached(i):
            copy.start()
    for copy in small:
        copy.wait()
    total = BLOCK * heads
    head = iota((total, 1), 0) % heads
    own_valid = iota((total, BLOCK), 0) // heads == iota((total, BLOCK), 1)
    lane = iota((heads, cache_len), 1)

    def block(step, carry):
        at = pl.ds(pl.multiple_of(step * BLOCK, BLOCK), BLOCK)
        q = q_buf[at, :].astype(jnp.float32)
        for h in range(heads):
            q_scr[pl.ds(h, BLOCK, stride=heads), :] = q[:, h * HEAD_DIM : (h + 1) * HEAD_DIM]
        q_all = q_scr[...]
        parts = [
            jnp.where((head >= k * group) & (head < (k + 1) * group), q_all, 0.0)
            for k in range(kv_local)
        ]
        q_bd = (parts[0] if kv_local == 1 else jnp.concatenate(parts, axis=1)).astype(jnp.bfloat16)
        own = lax.dot_general(q_bd, nk_buf[at, :], NT, preferred_element_type=jnp.float32)
        own = jnp.where(own_valid, own * scale, -1e30)
        key_copy, value_copy = cached(step)
        key_copy.wait()
        scores = jnp.concatenate(
            [
                jnp.where(
                    lane < len_ref[step * BLOCK + r],
                    lax.dot_general(
                        q_bd[r * heads : (r + 1) * heads],
                        k_buf[step * BLOCK + r],
                        NT,
                        preferred_element_type=jnp.float32,
                    )
                    * scale,
                    -1e30,
                )
                for r in range(BLOCK)
            ],
            axis=0,
        )
        highest = jnp.maximum(
            jnp.max(scores, axis=1, keepdims=True), jnp.max(own, axis=1, keepdims=True)
        )
        weights = jnp.exp(scores - highest)
        own_weights = jnp.exp(own - highest)
        inverse = 1.0 / (
            jnp.sum(weights, axis=1, keepdims=True) + jnp.sum(own_weights, axis=1, keepdims=True)
        )
        weights = (weights * inverse).astype(jnp.bfloat16)
        own_weights = (own_weights * inverse).astype(jnp.bfloat16)
        own_result = jnp.dot(own_weights, nv_buf[at, :], preferred_element_type=jnp.float32)
        value_copy.wait()
        for r in range(BLOCK):
            mine = slice(r * heads, (r + 1) * heads)
            result = own_result[mine] + jnp.dot(
                weights[mine], v_buf[step * BLOCK + r], preferred_element_type=jnp.float32
            )
            picked = result[:, :HEAD_DIM]
            for k in range(1, kv_local):
                picked = jnp.where(
                    head[:heads] >= k * group, result[:, k * HEAD_DIM : (k + 1) * HEAD_DIM], picked
                )
            o_scr[mine, :] = picked
        for h in range(heads):
            att_ref[at, h * HEAD_DIM : (h + 1) * HEAD_DIM] = o_scr[
                pl.ds(h, BLOCK, stride=heads), :
            ].astype(jnp.bfloat16)
        return carry

    lax.fori_loop(0, blocks, block, 0)
    _, home, rank = index_row(assign_ref[...], home_ref, var_local, dp_count)
    me = lax.axis_index("dp")
    over = (rank >= slot_refs[-1].shape[0]) & (home != me)
    flag = jnp.max(over.astype(jnp.float32), axis=1, keepdims=True)
    flag_ref[...] = jnp.broadcast_to(flag, flag_ref.shape).astype(jnp.bfloat16)
    attended = att_ref[...]
    for shift in range(dp_count):
        slot = iota((slot_refs[shift].shape[0], rows), 0)
        pick = (slot == rank) & (home == lax.rem(me + shift, dp_count))
        slot_refs[shift][...] = jnp.dot(
            one_hot(pick), attended, preferred_element_type=jnp.float32
        ).astype(jnp.bfloat16)


def attend(
    queries, new_keys, new_values, key_cache, value_cache, lengths, assign_row, home_index,
    var_local, slots,
):
    rows, width = queries.shape
    dp_count = len(slots)
    heads = width // HEAD_DIM
    blocks = rows // BLOCK
    vmem = pl.BlockSpec(memory_space=pltpu.VMEM)
    given = (queries, new_keys, new_values, key_cache, value_cache)
    return pl.pallas_call(
        functools.partial(attend_kernel, var_local, dp_count),
        in_specs=[pl.BlockSpec(memory_space=pltpu.HBM)] * 8,
        out_specs=[vmem] * (2 + dp_count),
        out_shape=[jax.ShapeDtypeStruct((rows, width), jnp.bfloat16)]
        + [jax.ShapeDtypeStruct((count, width), jnp.bfloat16) for count in slots]
        + [jax.ShapeDtypeStruct((16, 128), jnp.bfloat16)],
        scratch_shapes=[pltpu.VMEM(a.shape, a.dtype) for a in given]
        + [
            pltpu.SMEM(lengths.shape, jnp.int32),
            pltpu.VMEM(assign_row.shape, jnp.int32),
            pltpu.SMEM(home_index.shape, jnp.int32),
            pltpu.VMEM((BLOCK * heads, HEAD_DIM), jnp.float32),
            pltpu.VMEM((BLOCK * heads, HEAD_DIM), jnp.float32),
            pltpu.SemaphoreType.DMA((6,)),
            pltpu.SemaphoreType.DMA((blocks,)),
            pltpu.SemaphoreType.DMA((blocks,)),
        ],
        compiler_params=params(61),
        cost_estimate=FREE,
        name="attend",
    )(*given, lengths, assign_row, home_index)


def project_kernel(count, a_ref, w_hbm, *rest):
    outs, (w_buf, sem) = rest[:count], rest[count:]
    width = w_buf.shape[2]
    out_local = outs[0].shape[1]
    per = out_local // width
    me = lax.axis_index("tensor")
    order = [w for w in range(count) if w & 1] + [w for w in range(count) if not w & 1]

    def fetch(n):
        column = ((me ^ order[n // per]) * per + n % per) * width
        return pltpu.make_async_copy(
            w_hbm.at[:, pl.ds(pl.multiple_of(column, width), width)], w_buf.at[n], sem.at[n]
        )

    for n in range(count * per):
        fetch(n).start()
    attended = a_ref[...]
    for n in range(count * per):
        fetch(n).wait()
        at = slice(n % per * width, (n % per + 1) * width)
        outs[order[n // per]][:, at] = jnp.dot(
            attended, w_buf[n], preferred_element_type=jnp.float32
        ).astype(jnp.bfloat16)


def project(attended, out_weight, count, out_local):
    rows, depth = attended.shape
    width = min(512, out_local)
    tiles = out_weight.shape[1] // width
    vmem = pl.BlockSpec(memory_space=pltpu.VMEM)
    return pl.pallas_call(
        functools.partial(project_kernel, count),
        in_specs=[vmem, pl.BlockSpec(memory_space=pltpu.HBM)],
        out_specs=[vmem] * count,
        out_shape=[jax.ShapeDtypeStruct((rows, out_local), jnp.bfloat16)] * count,
        scratch_shapes=[
            pltpu.VMEM((tiles, depth, width), jnp.bfloat16),
            pltpu.SemaphoreType.DMA((tiles,)),
        ],
        compiler_params=params(44),
        cost_estimate=FREE,
        name="project",
    )(attended, out_weight)


def reduce_kernel(rows_ref, down_ref, flag_ref, there_ref, o_ref):
    wide = down_ref.shape[0]
    o_ref[:, :wide] = lax.dot_general(
        rows_ref[...], down_ref[...], NT, preferred_element_type=jnp.float32
    ).astype(o_ref.dtype)
    flag = jnp.maximum(flag_ref[...].astype(jnp.float32), there_ref[...].astype(jnp.float32))
    o_ref[:, wide:] = jnp.broadcast_to(flag[:1, :FLAG], (o_ref.shape[0], FLAG)).astype(o_ref.dtype)


def reduce_rows(rows, down, flag, flag_there):
    return pl.pallas_call(
        reduce_kernel,
        out_shape=jax.ShapeDtypeStruct((rows.shape[0], down.shape[0] + FLAG), jnp.bfloat16),
        compiler_params=params(8),
        cost_estimate=FREE,
        name="reduce_rows",
    )(rows, down, flag, flag_there)


def combine_kernel(var_local, dp_count, assign_ref, home_ref, *refs):
    o_ref, over_ref = refs[-2:]
    index = index_row(assign_ref[...], home_ref, var_local, dp_count)
    position, home, rank = [as_column(part) for part in index]
    rows, rank_width = o_ref.shape
    wide = refs[0].shape[1]
    total = jnp.zeros((rows, wide), jnp.float32)
    over = refs[0][:16, wide - FLAG :].astype(jnp.float32)
    for shift in range(dp_count):
        over = jnp.maximum(over, refs[shift][:16, wide - FLAG :].astype(jnp.float32))
        slot = iota((rows, refs[shift].shape[0]), 1)
        pick = (slot == rank) & (home == lax.rem(lax.axis_index("dp") + shift, dp_count))
        total = total + jnp.dot(one_hot(pick), refs[shift][...], preferred_element_type=jnp.float32)
    local = position - home * var_local
    start = local * rank_width
    lane = iota((rows, wide), 1)
    total = jnp.where((lane >= start) & (lane < start + rank_width), total, 0.0)
    low = total[:, :rank_width]
    for v in range(1, var_local):
        low = low + total[:, v * rank_width : (v + 1) * rank_width]
    o_ref[...] = low
    over_ref[...] = over[:8]


def combine(assign_row, home_index, parts, rank_width, var_local, dp_count):
    vmem = pl.BlockSpec(memory_space=pltpu.VMEM)
    return pl.pallas_call(
        functools.partial(combine_kernel, var_local, dp_count),
        in_specs=[vmem, pl.BlockSpec(memory_space=pltpu.SMEM)] + [vmem] * len(parts),
        out_specs=[vmem] * 2,
        out_shape=[
            jax.ShapeDtypeStruct((assign_row.shape[1], rank_width), jnp.float32),
            jax.ShapeDtypeStruct((8, FLAG), jnp.float32),
        ],
        compiler_params=params(8),
        cost_estimate=FREE,
        name="combine",
    )(assign_row, home_index, *parts)


def delta_kernel(var_local, dp_count, assign_ref, home_ref, low_ref, base_ref, add_ref, up_ref, *refs):
    o_ref = refs[-1]
    index = index_row(assign_ref[...], home_ref, var_local, dp_count)
    position = as_column(index[0])
    low = low_ref[...].astype(jnp.bfloat16)
    rows, rank_width = low.shape
    half = refs[0].shape[1]
    wide = up_ref.shape[0]
    spread = one_hot(iota((rank_width, wide), 1) % rank_width == iota((rank_width, wide), 0))
    low = jnp.dot(low, spread, preferred_element_type=jnp.float32)
    factor = iota((rows, wide), 1) // rank_width
    me = lax.axis_index("dp")
    last = dp_count - 1

    def factors(side, shift):
        if not side:
            return refs[shift - 1][...]
        if shift in (1, last):
            return refs[last][:wide] if shift == 1 else refs[last][wide:]
        return refs[last + shift - 1][...]

    def picked(shift):
        target = lax.rem(me + dp_count - shift, dp_count)
        return jnp.where(position == target * var_local + factor, low, 0.0).astype(jnp.bfloat16)

    mine = [picked(shift) for shift in range(dp_count)]
    for side in range(2):
        place = lax.rem(lax.axis_index("groups") + side, 2)
        columns = pl.ds(pl.multiple_of(place * half, half), half)
        total = jnp.dot(mine[0], up_ref[:, columns], preferred_element_type=jnp.float32)
        for shift in range(1, dp_count):
            total = total + jnp.dot(
                mine[shift], factors(side, shift), preferred_element_type=jnp.float32
            )
        base = base_ref[:, columns].astype(jnp.float32) + add_ref[:, columns].astype(jnp.float32)
        o_ref[:, columns] = (base + total).astype(jnp.bfloat16)


def add_delta(assign_row, home_index, low, base, add, up, others, var_local, dp_count):
    vmem = pl.BlockSpec(memory_space=pltpu.VMEM)
    return pl.pallas_call(
        functools.partial(delta_kernel, var_local, dp_count),
        in_specs=[vmem, pl.BlockSpec(memory_space=pltpu.SMEM)] + [vmem] * (4 + len(others)),
        out_specs=vmem,
        out_shape=jax.ShapeDtypeStruct(base.shape, jnp.bfloat16),
        compiler_params=params(16),
        cost_estimate=FREE,
        name="add_delta",
    )(assign_row, home_index, low, base, add, up, *others)


def per_device(
    queries, new_keys, new_values, key_cache, value_cache, lengths,
    out_weight, down_factors, up_factors, assignment, home_index,
):
    dp_count = lax.axis_size("dp")
    tensor_count = lax.axis_size("tensor")
    group_count = lax.axis_size("groups")
    t = lax.axis_index("tensor").astype(jnp.int32)
    y = lax.axis_index("groups").astype(jnp.int32)
    z = lax.axis_index("dp").astype(jnp.int32)
    rows = queries.shape[0]
    var_local, _, rank_width = down_factors.shape
    variants = var_local * dp_count
    out_local = up_factors.shape[2]
    capacity = max(2, 5 * rows // (2 * variants))
    most = min(rows, -(-var_local * capacity // 16) * 16)
    usual = min(most, -(-7 * rows // (4 * dp_count) // 8) * 8)
    bits = tensor_count.bit_length() - 1

    def along(values, axis, count, shift):
        return lax.ppermute(values, axis, [(i, (i + shift) % count) for i in range(count)])

    def across(values, bit):
        return lax.ppermute(
            values, "tensor", [(i, i ^ (1 << bit)) for i in range(tensor_count)]
        )

    half = out_local // 2
    up = up_factors.reshape(var_local * rank_width, out_local)
    piece = lax.dynamic_slice_in_dim(up, y * half, half, axis=1)
    near = {1: along(piece, "dp", dp_count, 1), dp_count - 1: along(piece, "dp", dp_count, -1)}

    assign_row = assignment[None, :]
    attended, *outgoing, flag = attend(
        queries, new_keys, new_values, key_cache, value_cache, lengths, assign_row, home_index,
        var_local, [most] + [usual] * (dp_count - 1),
    )
    last = dp_count - 1
    *outgoing[1:], flag = gate(61, outgoing[1:] + [flag], list(near.values()))
    flag_there = along(flag, "groups", group_count, 1)
    arrived = [outgoing[0]] + [
        along(outgoing[shift], "dp", dp_count, shift) for shift in range(1, dp_count)
    ]
    attended, near[1], near[last] = gate(
        1, [attended, near[1], near[last]], [flag_there]
    )
    far = {0: along(jnp.concatenate([near[1], near[last]]), "groups", group_count, 1)}
    for shift in range(2, last):
        near[shift] = along(near[shift - 1], "dp", dp_count, 1)
        far[shift] = along(near[shift], "groups", group_count, 1)

    held = dict(enumerate(project(attended, out_weight, tensor_count, out_local)))
    flags = [flag] * dp_count
    (flags[1],) = gate(1, [flag], [held[0]])
    for bit in range(bits):
        kept = {}
        for w in list(held):
            if w & (1 << bit):
                continue
            sent = held[w | (1 << bit)]
            got = across(sent, bit)
            if bit == bits - 1:
                add = got
                kept[w] = held[w]
            else:
                kept[w] = held[w].astype(jnp.float32) + got.astype(jnp.float32)
                if w:
                    kept[w] = kept[w].astype(jnp.bfloat16)
        held = kept

    down = jnp.swapaxes(down_factors, 1, 2).reshape(var_local * rank_width, -1)
    returned = []
    for shift in range(dp_count):
        part = reduce_rows(arrived[shift], down, flags[shift], flag_there)
        returned.append(part if shift == 0 else along(part, "dp", dp_count, -shift))

    returned[:1] = gate(1, returned[:1], [far[0], sent] + [near[shift] for shift in range(2, last)])

    def over_tensor(values):
        for bit in range(bits):
            values = values + across(values, bit)
        return values

    def with_rest(low):
        labels = jnp.arange(variants, dtype=jnp.int32)
        position = jnp.sum(
            jnp.where(assignment[:, None] == labels, home_index, 0), axis=1
        )
        home = position // var_local
        same = home[:, None] == jnp.arange(dp_count, dtype=jnp.int32)
        counted = jnp.cumsum(same.astype(jnp.int32), axis=0)
        rank = jnp.sum(jnp.where(same, counted, 0), axis=1) - 1
        slot = jnp.arange(most - usual, dtype=jnp.int32)[:, None] + usual
        rest = jnp.zeros((rows, var_local * rank_width), jnp.float32)
        for shift in range(1, dp_count):
            pick = (slot == rank) & (home == (z + shift) % dp_count)
            pick = pick.astype(jnp.bfloat16)
            sent = jnp.dot(pick, attended, preferred_element_type=jnp.float32)
            got = along(sent.astype(jnp.bfloat16), "dp", dp_count, shift)
            part = jnp.dot(got, down.T, preferred_element_type=jnp.float32).astype(jnp.bfloat16)
            part = along(part, "dp", dp_count, -shift)
            rest = rest + jnp.dot(pick.T, part, preferred_element_type=jnp.float32)
        rest = rest.reshape(rows, var_local, rank_width)
        local = (position - home * var_local)[:, None] == jnp.arange(var_local, dtype=jnp.int32)
        return low + over_tensor(jnp.sum(jnp.where(local[:, :, None], rest, 0.0), axis=1))

    low, over = combine(assign_row, home_index, returned, rank_width, var_local, dp_count)
    low = over_tensor(low)
    if usual < most:
        low = lax.cond(over[0, 0] > 0.5, with_rest, lambda low: low, low)
    middle = range(2, last)
    mixed = add_delta(
        assign_row, home_index, low, held[0], add, up,
        [near[1]] + [near[shift] for shift in middle] + [near[last], far[0]]
        + [far[shift] for shift in middle], var_local, dp_count,
    )

    pieces = {0: mixed}
    for bit in reversed(range(bits)):
        for w in list(pieces):
            pieces[w | (1 << bit)] = across(pieces[w], bit)
    whole = jnp.zeros((rows, tensor_count * out_local), jnp.bfloat16)
    for w, value in pieces.items():
        whole = lax.dynamic_update_slice(whole, value, (jnp.int32(0), (t ^ w) * out_local))
    return whole


def solution(mesh):
    placed = (
        P(("groups", "dp"), "tensor"),
        P(("groups", "dp"), "tensor"),
        P(("groups", "dp"), "tensor"),
        P(("groups", "dp"), None, "tensor"),
        P(("groups", "dp"), None, "tensor"),
        P(("groups", "dp")),
        P("tensor", None),
        P("dp", "tensor", None),
        P("dp", None, "tensor"),
        P(("groups", "dp")),
        P(),
    )
    return jax.shard_map(
        per_device, mesh=mesh, in_specs=placed, out_specs=P(("groups", "dp"), None), check_vma=False
    )
```

```python
import functools
import math

import jax
import jax.numpy as jnp
from jax import lax
from jax.experimental import pallas as pl
from jax.experimental.pallas import tpu as pltpu
from jax.sharding import PartitionSpec as P

HEAD_DIM = 128
BLOCK = 32
FLAG = 64
FREE = pl.CostEstimate(flops=0, bytes_accessed=0, transcendentals=0)
NT = (((1,), (1,)), ((), ()))


def params(mebibytes):
    return pltpu.CompilerParams(vmem_limit_bytes=mebibytes * 1024 * 1024)


def one_hot(mask):
    return mask.astype(jnp.float32).astype(jnp.bfloat16)


def iota(shape, axis):
    return lax.broadcasted_iota(jnp.int32, shape, axis)


def index_row(assign_row, home_ref, var_local, dp_count):
    rows = assign_row.shape[1]
    position = jnp.zeros((1, rows), jnp.int32)
    for v in range(var_local * dp_count):
        position = jnp.where(assign_row == v, home_ref[v], position)
    home = jnp.zeros((1, rows), jnp.int32)
    for d in range(1, dp_count):
        home = home + (position >= d * var_local).astype(jnp.int32)
    same = iota((max(16, dp_count), rows), 0) == home
    earlier = iota((rows, rows), 0) < iota((rows, rows), 1)
    before = jnp.dot(one_hot(same), one_hot(earlier), preferred_element_type=jnp.float32)
    rank = jnp.sum(jnp.where(same, before, 0.0), axis=0, keepdims=True)
    return position, home, rank.astype(jnp.int32)


def as_column(row):
    rows = row.shape[1]
    spread = jnp.where(iota((rows, rows), 0) == iota((rows, rows), 1), row.astype(jnp.float32), 0.0)
    return jnp.sum(spread, axis=1, keepdims=True).astype(jnp.int32)


def gate(mebibytes, values, ties):
    hbm = pl.BlockSpec(memory_space=pl.ANY)
    count = len(values)
    return pl.pallas_call(
        lambda *refs: None,
        in_specs=[hbm] * (count + len(ties)),
        out_specs=[hbm] * count,
        out_shape=[jax.ShapeDtypeStruct(v.shape, v.dtype) for v in values],
        input_output_aliases={i: i for i in range(count)},
        compiler_params=params(mebibytes),
        cost_estimate=FREE,
        name="gate",
    )(*values, *ties)


def attend_kernel(
    var_local, dp_count,
    q_hbm, nk_hbm, nv_hbm, k_hbm, v_hbm, len_hbm, assign_hbm, home_hbm, *rest
):
    att_ref = rest[0]
    slot_refs = rest[1 : 1 + dp_count]
    flag_ref = rest[1 + dp_count]
    (q_buf, nk_buf, nv_buf, k_buf, v_buf, len_ref, assign_ref, home_ref, q_scr, o_scr,
     small_sem, k_sem, v_sem) = rest[2 + dp_count :]
    rows, width = q_buf.shape
    cache_len = k_buf.shape[1]
    heads, kv_local = width // HEAD_DIM, nk_buf.shape[1] // HEAD_DIM
    group = heads // kv_local
    blocks = rows // BLOCK
    scale = 1.0 / math.sqrt(HEAD_DIM)
    small = [
        pltpu.make_async_copy(source, target, small_sem.at[i])
        for i, (source, target) in enumerate((
            (q_hbm, q_buf), (nk_hbm, nk_buf), (nv_hbm, nv_buf), (len_hbm, len_ref),
            (assign_hbm, assign_ref), (home_hbm, home_ref),
        ))
    ]

    def cached(i):
        at = pl.ds(i * BLOCK, BLOCK)
        return (
            pltpu.make_async_copy(k_hbm.at[at], k_buf.at[at], k_sem.at[i]),
            pltpu.make_async_copy(v_hbm.at[at], v_buf.at[at], v_sem.at[i]),
        )

    for copy in small:
        copy.start()
    for i in range(blocks):
        for copy in cached(i):
            copy.start()
    for copy in small:
        copy.wait()
    total = BLOCK * heads
    head = iota((total, 1), 0) % heads
    own_valid = iota((total, BLOCK), 0) // heads == iota((total, BLOCK), 1)
    lane = iota((heads, cache_len), 1)

    def block(step, carry):
        at = pl.ds(pl.multiple_of(step * BLOCK, BLOCK), BLOCK)
        q = q_buf[at, :].astype(jnp.float32)
        for h in range(heads):
            q_scr[pl.ds(h, BLOCK, stride=heads), :] = q[:, h * HEAD_DIM : (h + 1) * HEAD_DIM]
        q_all = q_scr[...]
        parts = [
            jnp.where((head >= k * group) & (head < (k + 1) * group), q_all, 0.0)
            for k in range(kv_local)
        ]
        q_bd = (parts[0] if kv_local == 1 else jnp.concatenate(parts, axis=1)).astype(jnp.bfloat16)
        own = lax.dot_general(q_bd, nk_buf[at, :], NT, preferred_element_type=jnp.float32)
        own = jnp.where(own_valid, own * scale, -1e30)
        key_copy, value_copy = cached(step)
        key_copy.wait()
        scores = jnp.concatenate(
            [
                jnp.where(
                    lane < len_ref[step * BLOCK + r],
                    lax.dot_general(
                        q_bd[r * heads : (r + 1) * heads],
                        k_buf[step * BLOCK + r],
                        NT,
                        preferred_element_type=jnp.float32,
                    )
                    * scale,
                    -1e30,
                )
                for r in range(BLOCK)
            ],
            axis=0,
        )
        highest = jnp.maximum(
            jnp.max(scores, axis=1, keepdims=True), jnp.max(own, axis=1, keepdims=True)
        )
        weights = jnp.exp(scores - highest)
        own_weights = jnp.exp(own - highest)
        inverse = 1.0 / (
            jnp.sum(weights, axis=1, keepdims=True) + jnp.sum(own_weights, axis=1, keepdims=True)
        )
        weights = (weights * inverse).astype(jnp.bfloat16)
        own_weights = (own_weights * inverse).astype(jnp.bfloat16)
        own_result = jnp.dot(own_weights, nv_buf[at, :], preferred_element_type=jnp.float32)
        value_copy.wait()
        for r in range(BLOCK):
            mine = slice(r * heads, (r + 1) * heads)
            result = own_result[mine] + jnp.dot(
                weights[mine], v_buf[step * BLOCK + r], preferred_element_type=jnp.float32
            )
            picked = result[:, :HEAD_DIM]
            for k in range(1, kv_local):
                picked = jnp.where(
                    head[:heads] >= k * group, result[:, k * HEAD_DIM : (k + 1) * HEAD_DIM], picked
                )
            o_scr[mine, :] = picked
        for h in range(heads):
            att_ref[at, h * HEAD_DIM : (h + 1) * HEAD_DIM] = o_scr[
                pl.ds(h, BLOCK, stride=heads), :
            ].astype(jnp.bfloat16)
        return carry

    lax.fori_loop(0, blocks, block, 0)
    _, home, rank = index_row(assign_ref[...], home_ref, var_local, dp_count)
    me = lax.axis_index("dp")
    over = (rank >= slot_refs[-1].shape[0]) & (home != me)
    flag = jnp.max(over.astype(jnp.float32), axis=1, keepdims=True)
    flag_ref[...] = jnp.broadcast_to(flag, flag_ref.shape).astype(jnp.bfloat16)
    attended = att_ref[...]
    for shift in range(dp_count):
        slot = iota((slot_refs[shift].shape[0], rows), 0)
        pick = (slot == rank) & (home == lax.rem(me + shift, dp_count))
        slot_refs[shift][...] = jnp.dot(
            one_hot(pick), attended, preferred_element_type=jnp.float32
        ).astype(jnp.bfloat16)


def attend(
    queries, new_keys, new_values, key_cache, value_cache, lengths, assign_row, home_index,
    var_local, slots,
):
    rows, width = queries.shape
    dp_count = len(slots)
    heads = width // HEAD_DIM
    blocks = rows // BLOCK
    vmem = pl.BlockSpec(memory_space=pltpu.VMEM)
    given = (queries, new_keys, new_values, key_cache, value_cache)
    return pl.pallas_call(
        functools.partial(attend_kernel, var_local, dp_count),
        in_specs=[pl.BlockSpec(memory_space=pltpu.HBM)] * 8,
        out_specs=[vmem] * (2 + dp_count),
        out_shape=[jax.ShapeDtypeStruct((rows, width), jnp.bfloat16)]
        + [jax.ShapeDtypeStruct((count, width), jnp.bfloat16) for count in slots]
        + [jax.ShapeDtypeStruct((16, 128), jnp.bfloat16)],
        scratch_shapes=[pltpu.VMEM(a.shape, a.dtype) for a in given]
        + [
            pltpu.SMEM(lengths.shape, jnp.int32),
            pltpu.VMEM(assign_row.shape, jnp.int32),
            pltpu.SMEM(home_index.shape, jnp.int32),
            pltpu.VMEM((BLOCK * heads, HEAD_DIM), jnp.float32),
            pltpu.VMEM((BLOCK * heads, HEAD_DIM), jnp.float32),
            pltpu.SemaphoreType.DMA((6,)),
            pltpu.SemaphoreType.DMA((blocks,)),
            pltpu.SemaphoreType.DMA((blocks,)),
        ],
        compiler_params=params(61),
        cost_estimate=FREE,
        name="attend",
    )(*given, lengths, assign_row, home_index)


def project_kernel(count, a_ref, w_hbm, *rest):
    outs, (w_buf, sem) = rest[:count], rest[count:]
    width = w_buf.shape[2]
    out_local = outs[0].shape[1]
    per = out_local // width
    me = lax.axis_index("tensor")
    order = list(reversed(range(count)))

    def fetch(n):
        column = ((me ^ order[n // per]) * per + n % per) * width
        return pltpu.make_async_copy(
            w_hbm.at[:, pl.ds(pl.multiple_of(column, width), width)], w_buf.at[n], sem.at[n]
        )

    for n in range(count * per):
        fetch(n).start()
    attended = a_ref[...]
    for n in range(count * per):
        fetch(n).wait()
        at = slice(n % per * width, (n % per + 1) * width)
        outs[order[n // per]][:, at] = jnp.dot(
            attended, w_buf[n], preferred_element_type=jnp.float32
        ).astype(jnp.bfloat16)


def project(attended, out_weight, count, out_local):
    rows, depth = attended.shape
    width = min(512, out_local)
    tiles = out_weight.shape[1] // width
    vmem = pl.BlockSpec(memory_space=pltpu.VMEM)
    return pl.pallas_call(
        functools.partial(project_kernel, count),
        in_specs=[vmem, pl.BlockSpec(memory_space=pltpu.HBM)],
        out_specs=[vmem] * count,
        out_shape=[jax.ShapeDtypeStruct((rows, out_local), jnp.bfloat16)] * count,
        scratch_shapes=[
            pltpu.VMEM((tiles, depth, width), jnp.bfloat16),
            pltpu.SemaphoreType.DMA((tiles,)),
        ],
        compiler_params=params(44),
        cost_estimate=FREE,
        name="project",
    )(attended, out_weight)


def reduce_kernel(rows_ref, down_ref, flag_ref, there_ref, o_ref):
    wide = down_ref.shape[0]
    o_ref[:, :wide] = lax.dot_general(
        rows_ref[...], down_ref[...], NT, preferred_element_type=jnp.float32
    ).astype(o_ref.dtype)
    flag = jnp.maximum(flag_ref[...].astype(jnp.float32), there_ref[...].astype(jnp.float32))
    o_ref[:, wide:] = jnp.broadcast_to(flag[:1, :FLAG], (o_ref.shape[0], FLAG)).astype(o_ref.dtype)


def reduce_rows(rows, down, flag, flag_there):
    return pl.pallas_call(
        reduce_kernel,
        out_shape=jax.ShapeDtypeStruct((rows.shape[0], down.shape[0] + FLAG), jnp.bfloat16),
        compiler_params=params(8),
        cost_estimate=FREE,
        name="reduce_rows",
    )(rows, down, flag, flag_there)


def combine_kernel(var_local, dp_count, assign_ref, home_ref, *refs):
    o_ref, over_ref = refs[-2:]
    index = index_row(assign_ref[...], home_ref, var_local, dp_count)
    position, home, rank = [as_column(part) for part in index]
    rows, rank_width = o_ref.shape
    wide = refs[0].shape[1]
    total = jnp.zeros((rows, wide), jnp.float32)
    over = refs[0][:16, wide - FLAG :].astype(jnp.float32)
    for shift in range(dp_count):
        over = jnp.maximum(over, refs[shift][:16, wide - FLAG :].astype(jnp.float32))
        slot = iota((rows, refs[shift].shape[0]), 1)
        pick = (slot == rank) & (home == lax.rem(lax.axis_index("dp") + shift, dp_count))
        total = total + jnp.dot(one_hot(pick), refs[shift][...], preferred_element_type=jnp.float32)
    local = position - home * var_local
    start = local * rank_width
    lane = iota((rows, wide), 1)
    total = jnp.where((lane >= start) & (lane < start + rank_width), total, 0.0)
    low = total[:, :rank_width]
    for v in range(1, var_local):
        low = low + total[:, v * rank_width : (v + 1) * rank_width]
    o_ref[...] = low
    over_ref[...] = over[:8]


def combine(assign_row, home_index, parts, rank_width, var_local, dp_count):
    vmem = pl.BlockSpec(memory_space=pltpu.VMEM)
    return pl.pallas_call(
        functools.partial(combine_kernel, var_local, dp_count),
        in_specs=[vmem, pl.BlockSpec(memory_space=pltpu.SMEM)] + [vmem] * len(parts),
        out_specs=[vmem] * 2,
        out_shape=[
            jax.ShapeDtypeStruct((assign_row.shape[1], rank_width), jnp.float32),
            jax.ShapeDtypeStruct((8, FLAG), jnp.float32),
        ],
        compiler_params=params(8),
        cost_estimate=FREE,
        name="combine",
    )(assign_row, home_index, *parts)


def delta_kernel(var_local, dp_count, assign_ref, home_ref, low_ref, base_ref, add_ref, up_ref, *refs):
    o_ref = refs[-1]
    index = index_row(assign_ref[...], home_ref, var_local, dp_count)
    position = as_column(index[0])
    low = low_ref[...].astype(jnp.bfloat16)
    rows, rank_width = low.shape
    half = refs[0].shape[1]
    wide = up_ref.shape[0]
    spread = one_hot(iota((rank_width, wide), 1) % rank_width == iota((rank_width, wide), 0))
    low = jnp.dot(low, spread, preferred_element_type=jnp.float32)
    factor = iota((rows, wide), 1) // rank_width
    me = lax.axis_index("dp")
    last = dp_count - 1

    def factors(side, shift):
        if not side:
            return refs[shift - 1][...]
        if shift in (1, last):
            return refs[last][:wide] if shift == 1 else refs[last][wide:]
        return refs[last + shift - 1][...]

    def picked(shift):
        target = lax.rem(me + dp_count - shift, dp_count)
        return jnp.where(position == target * var_local + factor, low, 0.0).astype(jnp.bfloat16)

    mine = [picked(shift) for shift in range(dp_count)]
    for side in range(2):
        place = lax.rem(lax.axis_index("groups") + side, 2)
        columns = pl.ds(pl.multiple_of(place * half, half), half)
        total = jnp.dot(mine[0], up_ref[:, columns], preferred_element_type=jnp.float32)
        for shift in range(1, dp_count):
            total = total + jnp.dot(
                mine[shift], factors(side, shift), preferred_element_type=jnp.float32
            )
        base = base_ref[:, columns].astype(jnp.float32) + add_ref[:, columns].astype(jnp.float32)
        o_ref[:, columns] = (base + total).astype(jnp.bfloat16)


def add_delta(assign_row, home_index, low, base, add, up, others, var_local, dp_count):
    vmem = pl.BlockSpec(memory_space=pltpu.VMEM)
    return pl.pallas_call(
        functools.partial(delta_kernel, var_local, dp_count),
        in_specs=[vmem, pl.BlockSpec(memory_space=pltpu.SMEM)] + [vmem] * (4 + len(others)),
        out_specs=vmem,
        out_shape=jax.ShapeDtypeStruct(base.shape, jnp.bfloat16),
        compiler_params=params(16),
        cost_estimate=FREE,
        name="add_delta",
    )(assign_row, home_index, low, base, add, up, *others)


def per_device(
    queries, new_keys, new_values, key_cache, value_cache, lengths,
    out_weight, down_factors, up_factors, assignment, home_index,
):
    dp_count = lax.axis_size("dp")
    tensor_count = lax.axis_size("tensor")
    group_count = lax.axis_size("groups")
    t = lax.axis_index("tensor").astype(jnp.int32)
    y = lax.axis_index("groups").astype(jnp.int32)
    z = lax.axis_index("dp").astype(jnp.int32)
    rows = queries.shape[0]
    var_local, _, rank_width = down_factors.shape
    variants = var_local * dp_count
    out_local = up_factors.shape[2]
    capacity = max(2, 5 * rows // (2 * variants))
    most = min(rows, -(-var_local * capacity // 16) * 16)
    usual = min(most, -(-7 * rows // (4 * dp_count) // 8) * 8)
    bits = tensor_count.bit_length() - 1

    def along(values, axis, count, shift):
        return lax.ppermute(values, axis, [(i, (i + shift) % count) for i in range(count)])

    def across(values, bit):
        return lax.ppermute(
            values, "tensor", [(i, i ^ (1 << bit)) for i in range(tensor_count)]
        )

    half = out_local // 2
    up = up_factors.reshape(var_local * rank_width, out_local)
    piece = lax.dynamic_slice_in_dim(up, y * half, half, axis=1)
    near = {1: along(piece, "dp", dp_count, 1), dp_count - 1: along(piece, "dp", dp_count, -1)}

    assign_row = assignment[None, :]
    attended, *outgoing, flag = attend(
        queries, new_keys, new_values, key_cache, value_cache, lengths, assign_row, home_index,
        var_local, [most] + [usual] * (dp_count - 1),
    )
    last = dp_count - 1
    *outgoing[1:], flag = gate(61, outgoing[1:] + [flag], list(near.values()))
    flag_there = along(flag, "groups", group_count, 1)
    arrived = [outgoing[0]] + [
        along(outgoing[shift], "dp", dp_count, shift) for shift in range(1, dp_count)
    ]
    attended, near[1], near[last] = gate(
        1, [attended, near[1], near[last]], [flag_there]
    )
    far = {0: along(jnp.concatenate([near[1], near[last]]), "groups", group_count, 1)}
    for shift in range(2, last):
        near[shift] = along(near[shift - 1], "dp", dp_count, 1)
        far[shift] = along(near[shift], "groups", group_count, 1)

    held = dict(enumerate(project(attended, out_weight, tensor_count, out_local)))
    flags = [flag] * dp_count
    (flags[1],) = gate(1, [flag], [held[0]])
    for bit in reversed(range(bits)):
        kept = {}
        for w in list(held):
            if w & (1 << bit):
                continue
            sent = held[w | (1 << bit)]
            got = across(sent, bit)
            if bit == 0:
                add = got
                kept[w] = held[w]
            else:
                kept[w] = held[w].astype(jnp.float32) + got.astype(jnp.float32)
                if w:
                    kept[w] = kept[w].astype(jnp.bfloat16)
        held = kept

    down = jnp.swapaxes(down_factors, 1, 2).reshape(var_local * rank_width, -1)
    returned = []
    for shift in range(dp_count):
        part = reduce_rows(arrived[shift], down, flags[shift], flag_there)
        returned.append(part if shift == 0 else along(part, "dp", dp_count, -shift))

    returned[:1] = gate(1, returned[:1], [far[0], sent] + [near[shift] for shift in range(2, last)])

    def over_tensor(values):
        for bit in range(bits):
            values = values + across(values, bit)
        return values

    def with_rest(low):
        labels = jnp.arange(variants, dtype=jnp.int32)
        position = jnp.sum(
            jnp.where(assignment[:, None] == labels, home_index, 0), axis=1
        )
        home = position // var_local
        same = home[:, None] == jnp.arange(dp_count, dtype=jnp.int32)
        counted = jnp.cumsum(same.astype(jnp.int32), axis=0)
        rank = jnp.sum(jnp.where(same, counted, 0), axis=1) - 1
        slot = jnp.arange(most - usual, dtype=jnp.int32)[:, None] + usual
        rest = jnp.zeros((rows, var_local * rank_width), jnp.float32)
        for shift in range(1, dp_count):
            pick = (slot == rank) & (home == (z + shift) % dp_count)
            pick = pick.astype(jnp.bfloat16)
            sent = jnp.dot(pick, attended, preferred_element_type=jnp.float32)
            got = along(sent.astype(jnp.bfloat16), "dp", dp_count, shift)
            part = jnp.dot(got, down.T, preferred_element_type=jnp.float32).astype(jnp.bfloat16)
            part = along(part, "dp", dp_count, -shift)
            rest = rest + jnp.dot(pick.T, part, preferred_element_type=jnp.float32)
        rest = rest.reshape(rows, var_local, rank_width)
        local = (position - home * var_local)[:, None] == jnp.arange(var_local, dtype=jnp.int32)
        return low + over_tensor(jnp.sum(jnp.where(local[:, :, None], rest, 0.0), axis=1))

    low, over = combine(assign_row, home_index, returned, rank_width, var_local, dp_count)
    low = over_tensor(low)
    if usual < most:
        low = lax.cond(over[0, 0] > 0.5, with_rest, lambda low: low, low)
    middle = range(2, last)
    mixed = add_delta(
        assign_row, home_index, low, held[0], add, up,
        [near[1]] + [near[shift] for shift in middle] + [near[last], far[0]]
        + [far[shift] for shift in middle], var_local, dp_count,
    )

    pieces = {0: mixed}
    for bit in reversed(range(bits)):
        for w in list(pieces):
            pieces[w | (1 << bit)] = across(pieces[w], bit)
    whole = jnp.zeros((rows, tensor_count * out_local), jnp.bfloat16)
    for w, value in pieces.items():
        whole = lax.dynamic_update_slice(whole, value, (jnp.int32(0), (t ^ w) * out_local))
    return whole


def solution(mesh):
    placed = (
        P(("groups", "dp"), "tensor"),
        P(("groups", "dp"), "tensor"),
        P(("groups", "dp"), "tensor"),
        P(("groups", "dp"), None, "tensor"),
        P(("groups", "dp"), None, "tensor"),
        P(("groups", "dp")),
        P("tensor", None),
        P("dp", "tensor", None),
        P("dp", None, "tensor"),
        P(("groups", "dp")),
        P(),
    )
    return jax.shard_map(
        per_device, mesh=mesh, in_specs=placed, out_specs=P(("groups", "dp"), None), check_vma=False
    )
```

```python
import functools
import math

import jax
import jax.numpy as jnp
from jax import lax
from jax.experimental import pallas as pl
from jax.experimental.pallas import tpu as pltpu
from jax.sharding import PartitionSpec as P

HEAD_DIM = 128
BLOCK = 32
FLAG = 64
FREE = pl.CostEstimate(flops=0, bytes_accessed=0, transcendentals=0)
NT = (((1,), (1,)), ((), ()))


def params(mebibytes):
    return pltpu.CompilerParams(vmem_limit_bytes=mebibytes * 1024 * 1024)


def one_hot(mask):
    return mask.astype(jnp.float32).astype(jnp.bfloat16)


def iota(shape, axis):
    return lax.broadcasted_iota(jnp.int32, shape, axis)


def index_row(assign_row, home_ref, var_local, dp_count):
    rows = assign_row.shape[1]
    position = jnp.zeros((1, rows), jnp.int32)
    for v in range(var_local * dp_count):
        position = jnp.where(assign_row == v, home_ref[v], position)
    home = jnp.zeros((1, rows), jnp.int32)
    for d in range(1, dp_count):
        home = home + (position >= d * var_local).astype(jnp.int32)
    same = iota((max(16, dp_count), rows), 0) == home
    earlier = iota((rows, rows), 0) < iota((rows, rows), 1)
    before = jnp.dot(one_hot(same), one_hot(earlier), preferred_element_type=jnp.float32)
    rank = jnp.sum(jnp.where(same, before, 0.0), axis=0, keepdims=True)
    return position, home, rank.astype(jnp.int32)


def as_column(row):
    rows = row.shape[1]
    spread = jnp.where(iota((rows, rows), 0) == iota((rows, rows), 1), row.astype(jnp.float32), 0.0)
    return jnp.sum(spread, axis=1, keepdims=True).astype(jnp.int32)


def gate(mebibytes, values, ties):
    hbm = pl.BlockSpec(memory_space=pl.ANY)
    count = len(values)
    return pl.pallas_call(
        lambda *refs: None,
        in_specs=[hbm] * (count + len(ties)),
        out_specs=[hbm] * count,
        out_shape=[jax.ShapeDtypeStruct(v.shape, v.dtype) for v in values],
        input_output_aliases={i: i for i in range(count)},
        compiler_params=params(mebibytes),
        cost_estimate=FREE,
        name="gate",
    )(*values, *ties)


def attend_kernel(
    var_local, dp_count,
    q_hbm, nk_hbm, nv_hbm, k_hbm, v_hbm, len_hbm, assign_hbm, home_hbm, *rest
):
    att_ref = rest[0]
    slot_refs = rest[1 : 1 + dp_count]
    flag_ref = rest[1 + dp_count]
    (q_buf, nk_buf, nv_buf, k_buf, v_buf, len_ref, assign_ref, home_ref, q_scr, o_scr,
     small_sem, k_sem, v_sem) = rest[2 + dp_count :]
    rows, width = q_buf.shape
    cache_len = k_buf.shape[1]
    heads, kv_local = width // HEAD_DIM, nk_buf.shape[1] // HEAD_DIM
    group = heads // kv_local
    blocks = rows // BLOCK
    scale = 1.0 / math.sqrt(HEAD_DIM)
    small = [
        pltpu.make_async_copy(source, target, small_sem.at[i])
        for i, (source, target) in enumerate((
            (q_hbm, q_buf), (nk_hbm, nk_buf), (nv_hbm, nv_buf), (len_hbm, len_ref),
            (assign_hbm, assign_ref), (home_hbm, home_ref),
        ))
    ]

    def cached(i):
        at = pl.ds(i * BLOCK, BLOCK)
        return (
            pltpu.make_async_copy(k_hbm.at[at], k_buf.at[at], k_sem.at[i]),
            pltpu.make_async_copy(v_hbm.at[at], v_buf.at[at], v_sem.at[i]),
        )

    for copy in small:
        copy.start()
    for i in range(blocks):
        for copy in cached(i):
            copy.start()
    for copy in small:
        copy.wait()
    total = BLOCK * heads
    head = iota((total, 1), 0) % heads
    own_valid = iota((total, BLOCK), 0) // heads == iota((total, BLOCK), 1)
    lane = iota((heads, cache_len), 1)

    def block(step, carry):
        at = pl.ds(pl.multiple_of(step * BLOCK, BLOCK), BLOCK)
        q = q_buf[at, :].astype(jnp.float32)
        for h in range(heads):
            q_scr[pl.ds(h, BLOCK, stride=heads), :] = q[:, h * HEAD_DIM : (h + 1) * HEAD_DIM]
        q_all = q_scr[...]
        parts = [
            jnp.where((head >= k * group) & (head < (k + 1) * group), q_all, 0.0)
            for k in range(kv_local)
        ]
        q_bd = (parts[0] if kv_local == 1 else jnp.concatenate(parts, axis=1)).astype(jnp.bfloat16)
        own = lax.dot_general(q_bd, nk_buf[at, :], NT, preferred_element_type=jnp.float32)
        own = jnp.where(own_valid, own * scale, -1e30)
        key_copy, value_copy = cached(step)
        key_copy.wait()
        scores = jnp.concatenate(
            [
                jnp.where(
                    lane < len_ref[step * BLOCK + r],
                    lax.dot_general(
                        q_bd[r * heads : (r + 1) * heads],
                        k_buf[step * BLOCK + r],
                        NT,
                        preferred_element_type=jnp.float32,
                    )
                    * scale,
                    -1e30,
                )
                for r in range(BLOCK)
            ],
            axis=0,
        )
        highest = jnp.maximum(
            jnp.max(scores, axis=1, keepdims=True), jnp.max(own, axis=1, keepdims=True)
        )
        weights = jnp.exp(scores - highest)
        own_weights = jnp.exp(own - highest)
        inverse = 1.0 / (
            jnp.sum(weights, axis=1, keepdims=True) + jnp.sum(own_weights, axis=1, keepdims=True)
        )
        weights = (weights * inverse).astype(jnp.bfloat16)
        own_weights = (own_weights * inverse).astype(jnp.bfloat16)
        own_result = jnp.dot(own_weights, nv_buf[at, :], preferred_element_type=jnp.float32)
        value_copy.wait()
        for r in range(BLOCK):
            mine = slice(r * heads, (r + 1) * heads)
            result = own_result[mine] + jnp.dot(
                weights[mine], v_buf[step * BLOCK + r], preferred_element_type=jnp.float32
            )
            picked = result[:, :HEAD_DIM]
            for k in range(1, kv_local):
                picked = jnp.where(
                    head[:heads] >= k * group, result[:, k * HEAD_DIM : (k + 1) * HEAD_DIM], picked
                )
            o_scr[mine, :] = picked
        for h in range(heads):
            att_ref[at, h * HEAD_DIM : (h + 1) * HEAD_DIM] = o_scr[
                pl.ds(h, BLOCK, stride=heads), :
            ].astype(jnp.bfloat16)
        return carry

    lax.fori_loop(0, blocks, block, 0)
    _, home, rank = index_row(assign_ref[...], home_ref, var_local, dp_count)
    me = lax.axis_index("dp")
    over = (rank >= slot_refs[-1].shape[0]) & (home != me)
    flag = jnp.max(over.astype(jnp.float32), axis=1, keepdims=True)
    flag_ref[...] = jnp.broadcast_to(flag, flag_ref.shape).astype(jnp.bfloat16)
    attended = att_ref[...]
    for shift in range(dp_count):
        slot = iota((slot_refs[shift].shape[0], rows), 0)
        pick = (slot == rank) & (home == lax.rem(me + shift, dp_count))
        slot_refs[shift][...] = jnp.dot(
            one_hot(pick), attended, preferred_element_type=jnp.float32
        ).astype(jnp.bfloat16)


def attend(
    queries, new_keys, new_values, key_cache, value_cache, lengths, assign_row, home_index,
    var_local, slots,
):
    rows, width = queries.shape
    dp_count = len(slots)
    heads = width // HEAD_DIM
    blocks = rows // BLOCK
    vmem = pl.BlockSpec(memory_space=pltpu.VMEM)
    given = (queries, new_keys, new_values, key_cache, value_cache)
    return pl.pallas_call(
        functools.partial(attend_kernel, var_local, dp_count),
        in_specs=[pl.BlockSpec(memory_space=pltpu.HBM)] * 8,
        out_specs=[vmem] * (2 + dp_count),
        out_shape=[jax.ShapeDtypeStruct((rows, width), jnp.bfloat16)]
        + [jax.ShapeDtypeStruct((count, width), jnp.bfloat16) for count in slots]
        + [jax.ShapeDtypeStruct((16, 128), jnp.bfloat16)],
        scratch_shapes=[pltpu.VMEM(a.shape, a.dtype) for a in given]
        + [
            pltpu.SMEM(lengths.shape, jnp.int32),
            pltpu.VMEM(assign_row.shape, jnp.int32),
            pltpu.SMEM(home_index.shape, jnp.int32),
            pltpu.VMEM((BLOCK * heads, HEAD_DIM), jnp.float32),
            pltpu.VMEM((BLOCK * heads, HEAD_DIM), jnp.float32),
            pltpu.SemaphoreType.DMA((6,)),
            pltpu.SemaphoreType.DMA((blocks,)),
            pltpu.SemaphoreType.DMA((blocks,)),
        ],
        compiler_params=params(61),
        cost_estimate=FREE,
        name="attend",
    )(*given, lengths, assign_row, home_index)


def project_kernel(count, a_ref, w_hbm, *rest):
    outs, (w_buf, sem) = rest[:count], rest[count:]
    width = w_buf.shape[2]
    out_local = outs[0].shape[1]
    per = out_local // width
    me = lax.axis_index("tensor")
    order = list(reversed(range(count)))

    def fetch(n):
        column = ((me ^ order[n // per]) * per + n % per) * width
        return pltpu.make_async_copy(
            w_hbm.at[:, pl.ds(pl.multiple_of(column, width), width)], w_buf.at[n], sem.at[n]
        )

    for n in range(count * per):
        fetch(n).start()
    attended = a_ref[...]
    for n in range(count * per):
        fetch(n).wait()
        at = slice(n % per * width, (n % per + 1) * width)
        outs[order[n // per]][:, at] = jnp.dot(
            attended, w_buf[n], preferred_element_type=jnp.float32
        ).astype(jnp.bfloat16)


def project(attended, out_weight, count, out_local):
    rows, depth = attended.shape
    width = min(512, out_local)
    tiles = out_weight.shape[1] // width
    vmem = pl.BlockSpec(memory_space=pltpu.VMEM)
    return pl.pallas_call(
        functools.partial(project_kernel, count),
        in_specs=[vmem, pl.BlockSpec(memory_space=pltpu.HBM)],
        out_specs=[vmem] * count,
        out_shape=[jax.ShapeDtypeStruct((rows, out_local), jnp.bfloat16)] * count,
        scratch_shapes=[
            pltpu.VMEM((tiles, depth, width), jnp.bfloat16),
            pltpu.SemaphoreType.DMA((tiles,)),
        ],
        compiler_params=params(44),
        cost_estimate=FREE,
        name="project",
    )(attended, out_weight)


def reduce_kernel(rows_ref, down_ref, flag_ref, there_ref, o_ref):
    wide = down_ref.shape[0]
    o_ref[:, :wide] = lax.dot_general(
        rows_ref[...], down_ref[...], NT, preferred_element_type=jnp.float32
    ).astype(o_ref.dtype)
    flag = jnp.maximum(flag_ref[...].astype(jnp.float32), there_ref[...].astype(jnp.float32))
    o_ref[:, wide:] = jnp.broadcast_to(flag[:1, :FLAG], (o_ref.shape[0], FLAG)).astype(o_ref.dtype)


def reduce_rows(rows, down, flag, flag_there):
    return pl.pallas_call(
        reduce_kernel,
        out_shape=jax.ShapeDtypeStruct((rows.shape[0], down.shape[0] + FLAG), jnp.bfloat16),
        compiler_params=params(8),
        cost_estimate=FREE,
        name="reduce_rows",
    )(rows, down, flag, flag_there)


def reduce_own_kernel(
    var_local, dp_count, rows_ref, down_ref, flag_ref, there_ref, assign_ref, home_ref,
    o_ref, position_ref, local_ref, *pick_refs
):
    reduce_kernel(rows_ref, down_ref, flag_ref, there_ref, o_ref)
    index = index_row(assign_ref[...], home_ref, var_local, dp_count)
    position, home, rank = [as_column(part) for part in index]
    position_ref[...] = jnp.broadcast_to(position, position_ref.shape)
    local_ref[...] = jnp.broadcast_to(position - home * var_local, local_ref.shape)
    for shift, pick_ref in enumerate(pick_refs):
        target = lax.rem(lax.axis_index("dp") + shift, dp_count)
        pick_ref[...] = one_hot((iota(pick_ref.shape, 1) == rank) & (home == target))


def reduce_own(rows, down, flag, flag_there, assign_row, home_index, var_local, slots):
    vmem = pl.BlockSpec(memory_space=pltpu.VMEM)
    requests = assign_row.shape[1]
    return pl.pallas_call(
        functools.partial(reduce_own_kernel, var_local, len(slots)),
        in_specs=[vmem] * 5 + [pl.BlockSpec(memory_space=pltpu.SMEM)],
        out_specs=[vmem] * (3 + len(slots)),
        out_shape=[jax.ShapeDtypeStruct((rows.shape[0], down.shape[0] + FLAG), jnp.bfloat16)]
        + [jax.ShapeDtypeStruct((requests, 128), jnp.int32)] * 2
        + [jax.ShapeDtypeStruct((requests, count), jnp.bfloat16) for count in slots],
        compiler_params=params(8),
        cost_estimate=FREE,
        name="reduce_own",
    )(rows, down, flag, flag_there, assign_row, home_index)


def combine_kernel(var_local, dp_count, local_ref, *refs):
    o_ref, over_ref = refs[-2:]
    pick_refs, part_refs = refs[:dp_count], refs[dp_count:-2]
    rows, rank_width = o_ref.shape
    wide = part_refs[0].shape[1]
    total = jnp.zeros((rows, wide), jnp.float32)
    over = part_refs[0][:16, wide - FLAG :].astype(jnp.float32)
    for pick_ref, part_ref in zip(pick_refs, part_refs):
        over = jnp.maximum(over, part_ref[:16, wide - FLAG :].astype(jnp.float32))
        total = total + jnp.dot(pick_ref[...], part_ref[...], preferred_element_type=jnp.float32)
    start = local_ref[:, :1] * rank_width
    lane = iota((rows, wide), 1)
    total = jnp.where((lane >= start) & (lane < start + rank_width), total, 0.0)
    low = total[:, :rank_width]
    for v in range(1, var_local):
        low = low + total[:, v * rank_width : (v + 1) * rank_width]
    o_ref[...] = low
    over_ref[...] = over[:8]


def combine(local, picks, parts, rank_width, var_local):
    vmem = pl.BlockSpec(memory_space=pltpu.VMEM)
    return pl.pallas_call(
        functools.partial(combine_kernel, var_local, len(parts)),
        in_specs=[vmem] * (1 + 2 * len(parts)),
        out_specs=[vmem] * 2,
        out_shape=[
            jax.ShapeDtypeStruct((local.shape[0], rank_width), jnp.float32),
            jax.ShapeDtypeStruct((8, FLAG), jnp.float32),
        ],
        compiler_params=params(8),
        cost_estimate=FREE,
        name="combine",
    )(local, *picks, *parts)


def delta_kernel(var_local, dp_count, position_ref, low_ref, base_ref, add_ref, up_ref, *refs):
    o_ref = refs[-1]
    position = position_ref[:, :1]
    low = low_ref[...].astype(jnp.bfloat16)
    rows, rank_width = low.shape
    half = refs[0].shape[1]
    wide = up_ref.shape[0]
    spread = one_hot(iota((rank_width, wide), 1) % rank_width == iota((rank_width, wide), 0))
    low = jnp.dot(low, spread, preferred_element_type=jnp.float32)
    factor = iota((rows, wide), 1) // rank_width
    me = lax.axis_index("dp")
    last = dp_count - 1

    def factors(side, shift):
        if not side:
            return refs[shift - 1][...]
        if shift in (1, last):
            return refs[last][:wide] if shift == 1 else refs[last][wide:]
        return refs[last + shift - 1][...]

    def picked(shift):
        target = lax.rem(me + dp_count - shift, dp_count)
        return jnp.where(position == target * var_local + factor, low, 0.0).astype(jnp.bfloat16)

    mine = [picked(shift) for shift in range(dp_count)]
    for side in range(2):
        place = lax.rem(lax.axis_index("groups") + side, 2)
        columns = pl.ds(pl.multiple_of(place * half, half), half)
        total = jnp.dot(mine[0], up_ref[:, columns], preferred_element_type=jnp.float32)
        for shift in range(1, dp_count):
            total = total + jnp.dot(
                mine[shift], factors(side, shift), preferred_element_type=jnp.float32
            )
        base = base_ref[:, columns].astype(jnp.float32) + add_ref[:, columns].astype(jnp.float32)
        o_ref[:, columns] = (base + total).astype(jnp.bfloat16)


def add_delta(position, low, base, add, up, others, var_local, dp_count):
    vmem = pl.BlockSpec(memory_space=pltpu.VMEM)
    return pl.pallas_call(
        functools.partial(delta_kernel, var_local, dp_count),
        in_specs=[vmem] * (5 + len(others)),
        out_specs=vmem,
        out_shape=jax.ShapeDtypeStruct(base.shape, jnp.bfloat16),
        compiler_params=params(16),
        cost_estimate=FREE,
        name="add_delta",
    )(position, low, base, add, up, *others)


def per_device(
    queries, new_keys, new_values, key_cache, value_cache, lengths,
    out_weight, down_factors, up_factors, assignment, home_index,
):
    dp_count = lax.axis_size("dp")
    tensor_count = lax.axis_size("tensor")
    group_count = lax.axis_size("groups")
    t = lax.axis_index("tensor").astype(jnp.int32)
    y = lax.axis_index("groups").astype(jnp.int32)
    z = lax.axis_index("dp").astype(jnp.int32)
    rows = queries.shape[0]
    var_local, _, rank_width = down_factors.shape
    variants = var_local * dp_count
    out_local = up_factors.shape[2]
    capacity = max(2, 5 * rows // (2 * variants))
    most = min(rows, -(-var_local * capacity // 16) * 16)
    usual = min(most, -(-7 * rows // (4 * dp_count) // 8) * 8)
    slots = [most] + [usual] * (dp_count - 1)
    bits = tensor_count.bit_length() - 1

    def along(values, axis, count, shift):
        return lax.ppermute(values, axis, [(i, (i + shift) % count) for i in range(count)])

    def across(values, bit):
        return lax.ppermute(
            values, "tensor", [(i, i ^ (1 << bit)) for i in range(tensor_count)]
        )

    half = out_local // 2
    up = up_factors.reshape(var_local * rank_width, out_local)
    piece = lax.dynamic_slice_in_dim(up, y * half, half, axis=1)
    near = {1: along(piece, "dp", dp_count, 1), dp_count - 1: along(piece, "dp", dp_count, -1)}

    assign_row = assignment[None, :]
    attended, *outgoing, flag = attend(
        queries, new_keys, new_values, key_cache, value_cache, lengths, assign_row, home_index,
        var_local, slots,
    )
    last = dp_count - 1
    *outgoing[1:], flag = gate(61, outgoing[1:] + [flag], list(near.values()))
    flag_there = along(flag, "groups", group_count, 1)
    arrived = [outgoing[0]] + [
        along(outgoing[shift], "dp", dp_count, shift) for shift in range(1, dp_count)
    ]
    attended, near[1], near[last] = gate(
        1, [attended, near[1], near[last]], [flag_there]
    )
    far = {0: along(jnp.concatenate([near[1], near[last]]), "groups", group_count, 1)}
    for shift in range(2, last):
        near[shift] = along(near[shift - 1], "dp", dp_count, 1)
        far[shift] = along(near[shift], "groups", group_count, 1)

    held = dict(enumerate(project(attended, out_weight, tensor_count, out_local)))
    flags = [flag] * dp_count
    (flags[1],) = gate(1, [flag], [held[0]])
    for bit in reversed(range(bits)):
        kept = {}
        for w in list(held):
            if w & (1 << bit):
                continue
            sent = held[w | (1 << bit)]
            got = across(sent, bit)
            if bit == 0:
                add = got
                kept[w] = held[w]
            else:
                kept[w] = held[w].astype(jnp.float32) + got.astype(jnp.float32)
                if w:
                    kept[w] = kept[w].astype(jnp.bfloat16)
        held = kept

    down = jnp.swapaxes(down_factors, 1, 2).reshape(var_local * rank_width, -1)
    own, position, local, *picks = reduce_own(
        arrived[0], down, flags[0], flag_there, assign_row, home_index, var_local, slots
    )
    returned = [own] + [
        along(reduce_rows(arrived[shift], down, flags[shift], flag_there), "dp", dp_count, -shift)
        for shift in range(1, dp_count)
    ]
    returned[:1] = gate(1, returned[:1], [far[0], sent] + [near[shift] for shift in range(2, last)])

    def over_tensor(values):
        for bit in range(bits):
            values = values + across(values, bit)
        return values

    def with_rest(low):
        labels = jnp.arange(variants, dtype=jnp.int32)
        position = jnp.sum(
            jnp.where(assignment[:, None] == labels, home_index, 0), axis=1
        )
        home = position // var_local
        same = home[:, None] == jnp.arange(dp_count, dtype=jnp.int32)
        counted = jnp.cumsum(same.astype(jnp.int32), axis=0)
        rank = jnp.sum(jnp.where(same, counted, 0), axis=1) - 1
        slot = jnp.arange(most - usual, dtype=jnp.int32)[:, None] + usual
        rest = jnp.zeros((rows, var_local * rank_width), jnp.float32)
        for shift in range(1, dp_count):
            pick = (slot == rank) & (home == (z + shift) % dp_count)
            pick = pick.astype(jnp.bfloat16)
            sent = jnp.dot(pick, attended, preferred_element_type=jnp.float32)
            got = along(sent.astype(jnp.bfloat16), "dp", dp_count, shift)
            part = jnp.dot(got, down.T, preferred_element_type=jnp.float32).astype(jnp.bfloat16)
            part = along(part, "dp", dp_count, -shift)
            rest = rest + jnp.dot(pick.T, part, preferred_element_type=jnp.float32)
        rest = rest.reshape(rows, var_local, rank_width)
        local = (position - home * var_local)[:, None] == jnp.arange(var_local, dtype=jnp.int32)
        return low + over_tensor(jnp.sum(jnp.where(local[:, :, None], rest, 0.0), axis=1))

    low, over = combine(local, picks, returned, rank_width, var_local)
    low = over_tensor(low)
    if usual < most:
        low = lax.cond(over[0, 0] > 0.5, with_rest, lambda low: low, low)
    middle = range(2, last)
    mixed = add_delta(
        position, low, held[0], add, up,
        [near[1]] + [near[shift] for shift in middle] + [near[last], far[0]]
        + [far[shift] for shift in middle], var_local, dp_count,
    )

    pieces = {0: mixed}
    for bit in reversed(range(bits)):
        for w in list(pieces):
            pieces[w | (1 << bit)] = across(pieces[w], bit)
    whole = jnp.zeros((rows, tensor_count * out_local), jnp.bfloat16)
    for w, value in pieces.items():
        whole = lax.dynamic_update_slice(whole, value, (jnp.int32(0), (t ^ w) * out_local))
    return whole


def solution(mesh):
    placed = (
        P(("groups", "dp"), "tensor"),
        P(("groups", "dp"), "tensor"),
        P(("groups", "dp"), "tensor"),
        P(("groups", "dp"), None, "tensor"),
        P(("groups", "dp"), None, "tensor"),
        P(("groups", "dp")),
        P("tensor", None),
        P("dp", "tensor", None),
        P("dp", None, "tensor"),
        P(("groups", "dp")),
        P(),
    )
    return jax.shard_map(
        per_device, mesh=mesh, in_specs=placed, out_specs=P(("groups", "dp"), None), check_vma=False
    )
```
